512 devices in a mesh: res: 32 (over z, x_lo), seq: 16 (over y, x_hi, core).
Axes of the slice: x: 4 (x_hi: 2, x_lo: 2; x = x_hi * 2 + x_lo), y: 4, z: 16, core: 2. Of those that a mesh axis runs over, the one named last changes fastest.
Arguments:
- alignment_input: bfloat16 [256, 1024, 256], P('seq', 'res'), may hold values from -8 to 8
- alignment_mask: int32 [256, 1024], P('seq', 'res'), may hold values from 0 to 1, as said below
- residue_present_mask: int32 [1024], P('res'), may hold values 0 or 1
- layer_norm_gain: float32 [256], replicated, may hold values from 0.1 to 1.9
- layer_norm_bias: float32 [256], replicated, may hold values from -3 to 3
- projection_weight: bfloat16 [256, 64], replicated, may hold values from -0.375 to 0.375
- projection_bias: float32 [64], replicated, may hold values from -4 to 4
- output_weight: bfloat16 [1024, 128], replicated, may hold values from -0.1875 to 0.1875
- output_bias: float32 [128], replicated, may hold values from -3 to 3
Outputs:
- pair_update: float32 [1024, 1024, 128], P('res', 'seq')
The draws below stay inside these ranges and needn't reach their ends.
Inputs may be any that keep to these rules, and one draw needn't show every extreme that they name: `alignment_mask`: 1 marks a present MSA entry.
All inputs are finite; a program needn't handle non-finite values. No bound on the sum of `residue_present_mask` on one device may be relied on, other than what follows from the above.
Results may differ from the reference program's by a relative error of at most 0.003.
Values may be sent and summed in bfloat16 or wider, within the bound.
No kernel may reach another device: no remote copies, remote signals or barrier semaphores. Data moves between devices by JAX's collectives and lax.ppermute only.
A program may use at most 64 MiB of HBM per device.

```python
import jax
import jax.numpy as jnp
from jax import lax

ALIGNMENT_WIDTH = 256
OUTER_CHANNELS = 32
PAIR_CH = 128
RES_DEV = 32
RESIDUE_COUNT = 1024
SEQUENCE_COUNT = 256
N_RES = 32


def draw_alignment_input(key, part):
    key = jax.random.fold_in(key, 11)
    profile_random_key, noise_random_key = jax.random.split(key, 2)
    channel_profile = jax.random.normal(profile_random_key, (RESIDUE_COUNT, ALIGNMENT_WIDTH), jnp.float32)
    noise_values = jax.random.normal(noise_random_key, (SEQUENCE_COUNT, RESIDUE_COUNT, ALIGNMENT_WIDTH), jnp.float32)
    value_array = channel_profile[None, :, :] + noise_values
    return jnp.clip(value_array, -8.0, 8.0).astype(jnp.bfloat16)


def draw_alignment_mask(key, part):
    key = jax.random.fold_in(key, 23)
    row_index = jnp.arange(SEQUENCE_COUNT, dtype=jnp.int32)
    thresholds = 400 - 280 * row_index // SEQUENCE_COUNT
    uniform_draws = jax.random.randint(key, (SEQUENCE_COUNT, RESIDUE_COUNT), 0, 1000, dtype=jnp.int32)
    return (uniform_draws < thresholds[:, None]).astype(jnp.int32)


def draw_output_bias(key, part):
    key = jax.random.fold_in(key, 37)
    magnitude_key = jax.random.fold_in(key, 0)
    bias_values = 1.2 * jax.random.normal(magnitude_key, (PAIR_CH,), jnp.float32)
    return jnp.clip(bias_values, -3.0, 3.0).astype(jnp.float32)


def place_ends(drawn, key, least, high):
    index_at = [jax.random.randint(jax.random.fold_in(key, axis), (), 0, length) for axis, length in enumerate(drawn.shape)]
    longest = drawn.shape.index(max(drawn.shape))
    beside = index_at[:longest] + [(index_at[longest] + 1) % drawn.shape[longest]] + index_at[longest + 1:]
    return drawn.at[tuple(index_at)].set(least).at[tuple(beside)].set(high)


def scatter_about(own_key, shape, deviation, limit, kind=jnp.bfloat16):
    values = deviation * jax.random.normal(own_key, shape, jnp.float32)
    return jnp.clip(values, min=-limit, max=limit).astype(kind)


def setup_inputs(seed: int = 0) -> dict:
    arg_keys = jax.random.split(jax.random.key(seed), 10)
    alignment_input = draw_alignment_input(jax.random.fold_in(arg_keys[9], 71), 0)
    alignment_mask = draw_alignment_mask(jax.random.fold_in(arg_keys[9], 71), 0)
    residue_present_mask = place_ends((jax.random.randint(arg_keys[2], (RESIDUE_COUNT,), 0, 8) < 7).astype(jnp.int32), jax.random.fold_in(arg_keys[2], 1), 0, 1)
    layer_norm_gain = jnp.clip(1.0 + 0.18 * jax.random.normal(arg_keys[3], (ALIGNMENT_WIDTH,), jnp.float32), 0.1, 1.9)
    layer_norm_bias = scatter_about(arg_keys[4], (ALIGNMENT_WIDTH,), 0.5, 3.0, jnp.float32)
    projection_weight = scatter_about(arg_keys[5], (ALIGNMENT_WIDTH, 2 * OUTER_CHANNELS), ALIGNMENT_WIDTH ** -0.5, 0.375)
    projection_bias = scatter_about(arg_keys[6], (2 * OUTER_CHANNELS,), 1.0, 4.0, jnp.float32)
    output_weight = scatter_about(arg_keys[7], (OUTER_CHANNELS * OUTER_CHANNELS, PAIR_CH), (OUTER_CHANNELS * OUTER_CHANNELS) ** -0.5, 0.1875)
    output_bias = draw_output_bias(jax.random.fold_in(arg_keys[9], 71), 0)
    return dict(alignment_input=alignment_input, alignment_mask=alignment_mask, residue_present_mask=residue_present_mask, layer_norm_gain=layer_norm_gain, layer_norm_bias=layer_norm_bias, projection_weight=projection_weight, projection_bias=projection_bias, output_weight=output_weight, output_bias=output_bias)


EPSILON = 1e-05

def project_alignment(alignment_input, alignment_mask, residue_present_mask, layer_norm_gain, layer_norm_bias, projection_weight, projection_bias):
    weight_array = (alignment_mask * residue_present_mask[None, :]).astype(jnp.float32)
    value_array = alignment_input.astype(jnp.float32)
    channel_mean = lax.optimization_barrier(jnp.mean(value_array, axis=-1, keepdims=True))
    centred = value_array - channel_mean
    channel_var = lax.optimization_barrier(jnp.mean(centred * centred, axis=-1, keepdims=True))
    normalized_input = (centred * lax.rsqrt(channel_var + EPSILON) * layer_norm_gain + layer_norm_bias).astype(jnp.bfloat16)
    sequence_total, residue_total, alignment_channels = alignment_input.shape
    projected_sides = jnp.dot(normalized_input.reshape(sequence_total * residue_total, alignment_channels), projection_weight, preferred_element_type=jnp.float32)
    projected_sides = projected_sides.reshape(sequence_total, residue_total, -1) + projection_bias
    projected_sides = (projected_sides * weight_array[:, :, None]).astype(jnp.bfloat16)
    return (projected_sides, weight_array)

def reference(alignment_input, alignment_mask, residue_present_mask, layer_norm_gain, layer_norm_bias, projection_weight, projection_bias, output_weight, output_bias):
    projected_sides, weight_array = project_alignment(alignment_input, alignment_mask, residue_present_mask, layer_norm_gain, layer_norm_bias, projection_weight, projection_bias)
    side_a = projected_sides[:, :, :OUTER_CHANNELS].astype(jnp.float32)
    side_b = projected_sides[:, :, OUTER_CHANNELS:].astype(jnp.float32)
    pair_count = jnp.dot(weight_array.T, weight_array, precision=lax.Precision.HIGHEST)

    def row_block(block_index):
        row_start = (block_index * RES_DEV).astype(jnp.int32)
        row_slice = lax.dynamic_slice_in_dim(side_a, row_start, RES_DEV, 1)
        outer_sum = jnp.einsum('sic,sjd->ijcd', row_slice, side_b, precision=lax.Precision.HIGHEST)
        outer_sum = outer_sum.reshape(RES_DEV * RESIDUE_COUNT, OUTER_CHANNELS * OUTER_CHANNELS).astype(jnp.bfloat16)
        update = jnp.dot(outer_sum, output_weight, preferred_element_type=jnp.float32)
        update = update.reshape(RES_DEV, RESIDUE_COUNT, PAIR_CH) + output_bias
        counts = lax.dynamic_slice_in_dim(pair_count, row_start, RES_DEV, 0)
        return update / jnp.maximum(counts, 1.0)[:, :, None]
    blocks = lax.map(row_block, jnp.arange(N_RES, dtype=jnp.int32))
    return blocks.reshape(RESIDUE_COUNT, RESIDUE_COUNT, PAIR_CH)
```

```python
import jax
import jax.numpy as jnp
from jax import lax
from jax.experimental import pallas as pl
from jax.experimental.pallas import tpu as pltpu
from jax.sharding import Mesh, PartitionSpec as P

EPSILON = 1e-05
SEQ = ("y", "xh", "core")
RES = ("z", "xl")


def project(x, mask, present, gain, bias, weight, proj_bias):
    weights = (mask * present[None, :]).astype(jnp.float32)
    value = x.astype(jnp.float32)
    mean = jnp.mean(value, axis=-1, keepdims=True)
    centred = value - mean
    var = jnp.mean(centred * centred, axis=-1, keepdims=True)
    normed = (centred * lax.rsqrt(var + EPSILON) * gain + bias).astype(jnp.bfloat16)
    s, r, w = x.shape
    proj = jnp.dot(normed.reshape(s * r, w), weight, preferred_element_type=jnp.float32)
    proj = proj.reshape(s, r, -1) + proj_bias
    return (proj * weights[:, :, None]).astype(jnp.bfloat16), weights.astype(jnp.bfloat16)


def pair_kernel(at_ref, b_ref, w_ref, bias_ref, o_ref, bint, xs):
    lane = lax.broadcasted_iota(jnp.int32, (256, 128), 1)
    odd = (lane // 32) % 2 == 1
    for g in range(8):
        v0 = b_ref[0, :, g * 128:(g + 1) * 128].astype(jnp.float32)
        v1 = b_ref[1, :, g * 128:(g + 1) * 128].astype(jnp.float32)
        bint[:, (2 * g) * 128:(2 * g + 1) * 128] = jnp.where(odd, pltpu.roll(v1, 32, 1), v0).astype(jnp.bfloat16)
        bint[:, (2 * g + 1) * 128:(2 * g + 2) * 128] = jnp.where(odd, v1, pltpu.roll(v0, 96, 1)).astype(jnp.bfloat16)
    w0 = b_ref[0, :, 1024:1152].astype(jnp.float32)
    w1 = b_ref[1, :, 1024:1152].astype(jnp.float32)
    wb = w0 + pltpu.roll(w1, 32, 1)
    wb = (wb + pltpu.roll(wb, 64, 1)).astype(jnp.bfloat16)
    count = jnp.dot(at_ref[1024:1056, :], wb, preferred_element_type=jnp.float32)
    low = lax.broadcasted_iota(jnp.int32, (16, 128), 1) < 64
    inv = 1.0 / jnp.maximum(jnp.where(low, count[:16], count[16:]), 1.0)
    bias = bias_ref[...]
    low = lax.broadcasted_iota(jnp.int32, (128, 128), 1) < 64
    for n in range(8):
        for m in range(4):
            o = jnp.dot(at_ref[m * 256:(m + 1) * 256, :], bint[:, n * 256:(n + 1) * 256],
                        preferred_element_type=jnp.float32).astype(jnp.bfloat16)
            for k in range(8):
                i = m * 8 + k
                for t in range(2):
                    h = 2 * n + t
                    xs[i // 2, h * 32:(h + 1) * 32, (i % 2) * 128:(i % 2 + 1) * 128] = (
                        o[k * 32:(k + 1) * 32, t * 128:(t + 1) * 128])
    for ip in range(16):
        y = jnp.dot(w_ref[...], xs[ip], preferred_element_type=jnp.float32)
        t0, b0, t1, b1 = y[:128, :128], y[128:, :128], y[:128, 128:], y[128:, 128:]
        u = jnp.where(low, t0, b1)
        v = jnp.where(low, t1, b0)
        z = (u + pltpu.roll(v, 64, 1) + bias) * inv[ip:ip + 1]
        zt = z.T
        o_ref[2 * ip] = zt[:64]
        o_ref[2 * ip + 1] = zt[64:]


def pair(at, b, w2, bias):
    return pl.pallas_call(
        pair_kernel,
        out_shape=jax.ShapeDtypeStruct((32, 64, 128), jnp.float32),
        in_specs=[pl.BlockSpec(memory_space=pltpu.VMEM)] * 4,
        out_specs=pl.BlockSpec(memory_space=pltpu.VMEM),
        scratch_shapes=[pltpu.VMEM((256, 2048), jnp.bfloat16), pltpu.VMEM((16, 512, 256), jnp.bfloat16)],
        compiler_params=pltpu.CompilerParams(vmem_limit_bytes=40 * 1024 * 1024),
        cost_estimate=pl.CostEstimate(flops=2 * 10**9, bytes_accessed=4 * 2**20, transcendentals=0),
        name="pair",
    )(at, b, w2, bias)


def local(x, mask, present, gain, bias, weight, proj_bias, out_weight, out_bias):
    proj, weights = project(x, mask, present, gain, bias, weight, proj_bias)
    s, r, _ = proj.shape
    zeros = jnp.zeros((s, 96), jnp.bfloat16)
    even_odd = weights.reshape(s, r // 2, 2).transpose(0, 2, 1).reshape(s, r)
    a = jnp.concatenate([proj[:, :, :32].reshape(s, r * 32), even_odd, zeros], axis=1)
    bt = proj[:, :, 32:].transpose(0, 2, 1).reshape(s, 8, 2, 2, r).transpose(0, 1, 3, 2, 4)
    b = jnp.concatenate([bt.reshape(s, r * 32), weights, zeros], axis=1)
    a_all = lax.all_to_all(jnp.broadcast_to(a[None], (16, *a.shape)), SEQ, 0, 0, tiled=True)
    b_z = lax.all_to_all(jnp.broadcast_to(b[None], (16, *b.shape)), "z", 0, 0, tiled=True)
    b_two = jnp.concatenate([b_z, b_z], axis=0)
    b_all = lax.all_to_all(b_two, ("xl",) + SEQ, 0, 0, tiled=True).reshape(2, 256, 1152)
    at = a_all.reshape(256, 1152).T
    w2 = out_weight.reshape(32, 16, 2, 128).transpose(2, 3, 1, 0).reshape(256, 512)
    bias2 = jnp.broadcast_to(out_bias[:, None], (128, 128))
    return pair(at, b_all, w2, bias2)


def solution(mesh):
    fine = Mesh(mesh.devices.reshape(16, 2, 4, 2, 2), ("z", "xl", "y", "xh", "core"))
    in_specs = (P(SEQ, RES, None), P(SEQ, RES), P(RES), P(), P(), P(), P(), P(), P())
    return jax.shard_map(local, mesh=fine, in_specs=in_specs, out_specs=P(RES, SEQ, None), check_vma=False)
```

```python
import jax
import jax.numpy as jnp
from jax import lax
from jax.experimental import pallas as pl
from jax.experimental.pallas import tpu as pltpu
from jax.sharding import Mesh, PartitionSpec as P

EPSILON = 1e-05
RES = ("z", "xl")
SEQ = ("y", "xh", "core")


def iota(shape, dim):
    return lax.broadcasted_iota(jnp.int32, shape, dim)


def ones_where(condition, dtype=jnp.bfloat16):
    return jnp.where(condition, 1.0, 0.0).astype(dtype)


def project_kernel(*refs):
    sources, (a_ref, b_ref), held, (pa, tiles, sems) = refs[:7], refs[7:9], refs[9:16], refs[16:]
    loads = [pltpu.make_async_copy(src, dst, sems.at[k]) for k, (src, dst) in enumerate(zip(sources, held))]
    for load in loads:
        load.start()
    for load in loads:
        load.wait()
    x_ref, mask_ref, present_ref, gain_ref, bias_ref, w_ref, pb_ref = held
    value = x_ref[...].reshape(512, 256).astype(jnp.float32)
    mean = jnp.mean(value, axis=-1, keepdims=True)
    centred = value - mean
    var = jnp.mean(centred * centred, axis=-1, keepdims=True)
    normed = (centred * lax.rsqrt(var + EPSILON) * gain_ref[...] + bias_ref[...]).astype(jnp.bfloat16)
    weights = (mask_ref[...] * present_ref[...]).astype(jnp.float32).astype(jnp.bfloat16)
    proj_w = w_ref[...]

    row, col = iota((32, 64), 0), iota((32, 64), 1)
    place = row // 8
    pick = ones_where(col == 32 + 4 * (row % 8) + (place % 2) * 2 + place // 2)
    wb = jnp.dot(pick, proj_w, preferred_element_type=jnp.float32)
    bt = lax.dot_general(wb.astype(jnp.bfloat16), normed, (((1,), (1,)), ((), ())), preferred_element_type=jnp.float32)
    row, col = iota((8, 64), 0), iota((8, 64), 1)
    own = jnp.where((col >= 32) & ((col - 32) // 4 == row), pb_ref[...], 0.0)
    row, lane = iota((64, 128), 0), iota((64, 128), 1) // 32
    spread = ones_where(row % 4 == (lane % 2) * 2 + lane // 2, jnp.float32)
    b_bias = jnp.dot(own, spread, precision=lax.Precision.HIGHEST, preferred_element_type=jnp.float32)
    group = iota((8, 128), 1) // 32
    for t in range(4):
        parts = [bt[p * 8:(p + 1) * 8, t * 128:(t + 1) * 128] for p in range(4)]
        for r in range(4):
            out = parts[r]
            for p in range(4):
                if p != r:
                    out = jnp.where(group == p, pltpu.roll(parts[p], (32 * (p - r)) % 128, 1), out)
            tiles[pl.ds(4 * t + r, 8, stride=16), :] = out + b_bias
    row, lane = iota((32, 128), 0), iota((32, 128), 1)
    b_weights = jnp.dot(weights, ones_where(lane % 32 == row), preferred_element_type=jnp.float32)
    for g in range(8):
        b_ref[g * 16:(g + 1) * 16, :] = (tiles[g * 16:(g + 1) * 16, :] * b_weights).astype(jnp.bfloat16)
    b_plain = jnp.where(iota((16, 128), 1) < 32, b_weights, 0.0)
    b_ref[128:136, :] = (b_plain[:8] + pltpu.roll(b_plain[8:], 64, 1)).astype(jnp.bfloat16)

    row, lane4 = iota((64, 128), 0), iota((64, 128), 1)
    four = ones_where(row == lane4 % 32)
    wa = lax.dot_general(four, proj_w, (((0,), (0,)), ((), ())), preferred_element_type=jnp.float32)
    a_bias = jnp.dot(jnp.broadcast_to(pb_ref[...], (8, 64)), four.astype(jnp.float32),
                     precision=lax.Precision.HIGHEST, preferred_element_type=jnp.float32)
    pa[...] = lax.dot_general(normed, wa.astype(jnp.bfloat16), (((1,), (1,)), ((), ())),
                              preferred_element_type=jnp.float32) + a_bias[0:1]
    group = iota((16, 128), 1) // 32
    for g in range(8):
        part = [pa[pl.ds(4 * g + k, 16, stride=32), :] for k in range(4)]
        out = jnp.where(group < 2, jnp.where(group == 0, part[0], part[1]), jnp.where(group == 2, part[2], part[3]))
        spread = jnp.dot(weights, ones_where(row[:32] == 4 * g + lane // 32), preferred_element_type=jnp.float32)
        a_ref[g * 16:(g + 1) * 16, :] = (out * spread).astype(jnp.bfloat16)
    even_odd = ones_where(lane == (row[:32] % 2) * 16 + row[:32] // 2)
    a_plain = jnp.dot(weights, even_odd, preferred_element_type=jnp.float32)
    a_ref[128:136, :] = (a_plain[:8] + pltpu.roll(a_plain[8:], 64, 1)).astype(jnp.bfloat16)


def project(x, mask, present, gain, bias, weight, proj_bias):
    vmem = pl.BlockSpec(memory_space=pltpu.VMEM)
    out = jax.ShapeDtypeStruct((136, 128), jnp.bfloat16)
    given = (x, mask, present[None], gain[None], bias[None], weight.T, proj_bias[None])
    return pl.pallas_call(
        project_kernel,
        out_shape=(out, out),
        in_specs=[pl.BlockSpec(memory_space=pl.ANY)] * 7,
        out_specs=(vmem, vmem),
        scratch_shapes=[pltpu.VMEM(g.shape, g.dtype) for g in given] + [
            pltpu.VMEM((512, 128), jnp.float32), pltpu.VMEM((128, 128), jnp.float32), pltpu.SemaphoreType.DMA((7,))],
        compiler_params=pltpu.CompilerParams(vmem_limit_bytes=56 * 1024 * 1024),
        cost_estimate=pl.CostEstimate(flops=4 * 10**7, bytes_accessed=2**19, transcendentals=0),
        name="project",
    )(*given)


def rows_kernel(pos_ref, own_ref, other_ref, at_ref, wa_ref, rows, packed):
    for k in range(16):
        src = own_ref if k < 8 else other_ref
        at = pos_ref[k]
        for g in range(8):
            rows[pl.ds(pl.multiple_of(at * 16, 16), 16), g * 128:(g + 1) * 128] = src[k % 8, g * 16:(g + 1) * 16, :]
        packed[pl.ds(pl.multiple_of(at * 8, 8), 8), :] = src[k % 8, 128:136, :].astype(jnp.float32)
    for g in range(8):
        at_ref[g * 128:(g + 1) * 128, :] = rows[:, g * 128:(g + 1) * 128].T
    wa_ref[...] = packed[...].astype(jnp.bfloat16)


def gather_rows(pos, own, other):
    vmem = pl.BlockSpec(memory_space=pltpu.VMEM)
    return pl.pallas_call(
        rows_kernel,
        out_shape=(jax.ShapeDtypeStruct((1024, 256), jnp.bfloat16), jax.ShapeDtypeStruct((128, 128), jnp.bfloat16)),
        in_specs=[pl.BlockSpec(memory_space=pltpu.SMEM), vmem, vmem],
        out_specs=(vmem, vmem),
        scratch_shapes=[pltpu.VMEM((256, 1024), jnp.bfloat16), pltpu.VMEM((128, 128), jnp.float32)],
        compiler_params=pltpu.CompilerParams(vmem_limit_bytes=16 * 1024 * 1024),
        cost_estimate=pl.CostEstimate(flops=10**6, bytes_accessed=2 * 2**20, transcendentals=0),
        name="rows",
    )(pos, own, other)


def pair_kernel(at_ref, wa_ref, b_ref, w_ref, bias_ref, o_ref, bint, xs):
    lane = iota((256, 128), 1)
    odd = (lane // 32) % 2 == 1
    for g in range(8):
        v0 = b_ref[0, :, g * 16:(g + 1) * 16, :].reshape(256, 128).astype(jnp.float32)
        v1 = b_ref[1, :, g * 16:(g + 1) * 16, :].reshape(256, 128).astype(jnp.float32)
        bint[:, (2 * g) * 128:(2 * g + 1) * 128] = jnp.where(odd, pltpu.roll(v1, 32, 1), v0).astype(jnp.bfloat16)
        bint[:, (2 * g + 1) * 128:(2 * g + 2) * 128] = jnp.where(odd, v1, pltpu.roll(v0, 96, 1)).astype(jnp.bfloat16)
    w0 = b_ref[0, :, 128:136, :].astype(jnp.float32).reshape(128, 128)
    w1 = b_ref[1, :, 128:136, :].astype(jnp.float32).reshape(128, 128)
    wb = (w0 + pltpu.roll(w1, 32, 1)).astype(jnp.bfloat16)
    count = lax.dot_general(wa_ref[...], wb, (((0,), (0,)), ((), ())), preferred_element_type=jnp.float32)
    count = count[0:32] + pltpu.roll(count[64:96], 64, 1)
    low = lax.broadcasted_iota(jnp.int32, (16, 128), 1) < 64
    inv = 1.0 / jnp.maximum(jnp.where(low, count[:16], pltpu.roll(count[16:], 64, 1)), 1.0)
    bias = bias_ref[...]
    low = lane[:128] < 64
    for n in range(8):
        for m in range(4):
            o = jnp.dot(at_ref[m * 256:(m + 1) * 256, :], bint[:, n * 256:(n + 1) * 256],
                        preferred_element_type=jnp.float32).astype(jnp.bfloat16)
            for k in range(8):
                i = m * 8 + k
                for t in range(2):
                    h = 2 * n + t
                    xs[i // 2, h * 32:(h + 1) * 32, (i % 2) * 128:(i % 2 + 1) * 128] = (
                        o[k * 32:(k + 1) * 32, t * 128:(t + 1) * 128])
    for ip in range(16):
        y = jnp.dot(w_ref[...], xs[ip], preferred_element_type=jnp.float32)
        t0, b0, t1, b1 = y[:128, :128], y[128:, :128], y[:128, 128:], y[128:, 128:]
        u = jnp.where(low, t0, b1)
        v = jnp.where(low, t1, b0)
        z = (u + pltpu.roll(v, 64, 1) + bias) * inv[ip:ip + 1]
        zt = z.T
        o_ref[2 * ip] = zt[:64]
        o_ref[2 * ip + 1] = zt[64:]


def pair(at, wa, b, w2, bias):
    return pl.pallas_call(
        pair_kernel,
        out_shape=jax.ShapeDtypeStruct((32, 64, 128), jnp.float32),
        in_specs=[pl.BlockSpec(memory_space=pltpu.VMEM)] * 5,
        out_specs=pl.BlockSpec(memory_space=pltpu.VMEM),
        scratch_shapes=[pltpu.VMEM((256, 2048), jnp.bfloat16), pltpu.VMEM((16, 512, 256), jnp.bfloat16)],
        compiler_params=pltpu.CompilerParams(vmem_limit_bytes=40 * 1024 * 1024),
        cost_estimate=pl.CostEstimate(flops=2 * 10**9, bytes_accessed=4 * 2**20, transcendentals=0),
        name="pair",
    )(at, wa, b, w2, bias)


def shift(n, by):
    return [(i, (i + by) % n) for i in range(n)]


def local(x, mask, present, gain, bias, weight, proj_bias, out_weight, out_bias):
    a, b = project(x, mask, present, gain, bias, weight, proj_bias)
    ax = lax.ppermute(a, "xh", shift(2, 1))
    b_z = lax.all_gather(b, "z")
    b_z, ax = lax.optimization_barrier((b_z, ax))
    b_two = jnp.broadcast_to(b_z[None], (2, *b_z.shape)).reshape(32, 136, 128)
    b_all = lax.all_to_all(b_two, ("xl",) + SEQ, 0, 0, tiled=True).reshape(2, 16, 136, 128)

    ay = [jnp.stack([a, ax])]
    for _ in range(3):
        ay.append(lax.ppermute(ay[-1], "y", shift(4, -1)))
    mine = jnp.concatenate(ay)
    other = lax.ppermute(mine, "core", shift(2, 1))
    y, xh, core = (lax.axis_index(n) for n in SEQ)
    pos = jnp.stack([
        ((y + k) % 4) * 4 + (xh ^ h) * 2 + (core ^ c) for c in range(2) for k in range(4) for h in range(2)
    ]).astype(jnp.int32)
    at, wa = gather_rows(pos, mine, other)

    w2 = out_weight.reshape(32, 16, 2, 128).transpose(2, 3, 1, 0).reshape(256, 512)
    bias2 = jnp.broadcast_to(out_bias[:, None], (128, 128))
    return pair(at, wa, b_all, w2, bias2)


def solution(mesh):
    fine = Mesh(mesh.devices.reshape(16, 2, 4, 2, 2), RES + SEQ)
    in_specs = (P(SEQ, RES, None), P(SEQ, RES), P(RES), P(), P(), P(), P(), P(), P())
    return jax.shard_map(local, mesh=fine, in_specs=in_specs, out_specs=P(RES, SEQ, None), check_vma=False)
```

```python
import jax
import jax.numpy as jnp
from jax import lax
from jax.experimental import pallas as pl
from jax.experimental.pallas import tpu as pltpu
from jax.sharding import Mesh, PartitionSpec as P

EPSILON = 1e-05
RES = ("z", "xl")
SEQ = ("y", "xh", "core")


def iota(shape, dim):
    return lax.broadcasted_iota(jnp.int32, shape, dim)


def ones_where(condition, dtype=jnp.bfloat16):
    return jnp.where(condition, 1.0, 0.0).astype(dtype)


def project_kernel(*refs):
    sources, (a_ref, b_ref), held, (pa, tiles, sems) = refs[:7], refs[7:9], refs[9:16], refs[16:]
    loads = [pltpu.make_async_copy(src, dst, sems.at[k]) for k, (src, dst) in enumerate(zip(sources, held))]
    for load in loads:
        load.start()
    for load in loads:
        load.wait()
    x_ref, mask_ref, present_ref, gain_ref, bias_ref, w_ref, pb_ref = held
    value = x_ref[...].reshape(512, 256).astype(jnp.float32)
    mean = jnp.mean(value, axis=-1, keepdims=True)
    centred = value - mean
    var = jnp.mean(centred * centred, axis=-1, keepdims=True)
    normed = (centred * lax.rsqrt(var + EPSILON) * gain_ref[...] + bias_ref[...]).astype(jnp.bfloat16)
    weights = (mask_ref[...] * present_ref[...]).astype(jnp.float32).astype(jnp.bfloat16)
    proj_w = w_ref[...]

    row, col = iota((32, 64), 0), iota((32, 64), 1)
    pick = ones_where(col == 32 + 4 * (row % 8) + row // 8)
    wb = jnp.dot(pick, proj_w, preferred_element_type=jnp.float32)
    bt = lax.dot_general(wb.astype(jnp.bfloat16), normed, (((1,), (1,)), ((), ())), preferred_element_type=jnp.float32)
    row, col = iota((8, 64), 0), iota((8, 64), 1)
    own = jnp.where((col >= 32) & ((col - 32) // 4 == row), pb_ref[...], 0.0)
    row, lane = iota((64, 128), 0), iota((64, 128), 1) // 32
    spread = ones_where(row % 4 == lane, jnp.float32)
    b_bias = jnp.dot(own, spread, precision=lax.Precision.HIGHEST, preferred_element_type=jnp.float32)
    group = iota((8, 128), 1) // 32
    for t in range(4):
        parts = [bt[p * 8:(p + 1) * 8, t * 128:(t + 1) * 128] for p in range(4)]
        for r in range(4):
            out = parts[r]
            for p in range(4):
                if p != r:
                    out = jnp.where(group == p, pltpu.roll(parts[p], (32 * (p - r)) % 128, 1), out)
            tiles[pl.ds(4 * t + r, 8, stride=16), :] = out + b_bias
    row, lane = iota((32, 128), 0), iota((32, 128), 1)
    b_weights = jnp.dot(weights, ones_where(lane % 32 == row), preferred_element_type=jnp.float32)
    for g in range(8):
        b_ref[g * 16:(g + 1) * 16, :] = (tiles[g * 16:(g + 1) * 16, :] * b_weights).astype(jnp.bfloat16)
    b_plain = jnp.where(iota((16, 128), 1) < 32, b_weights, 0.0)
    b_ref[128:136, :] = (b_plain[:8] + pltpu.roll(b_plain[8:], 64, 1)).astype(jnp.bfloat16)

    row, lane4 = iota((64, 128), 0), iota((64, 128), 1)
    four = ones_where(row == lane4 % 32)
    wa = lax.dot_general(four, proj_w, (((0,), (0,)), ((), ())), preferred_element_type=jnp.float32)
    a_bias = jnp.dot(jnp.broadcast_to(pb_ref[...], (8, 64)), four.astype(jnp.float32),
                     precision=lax.Precision.HIGHEST, preferred_element_type=jnp.float32)
    pa[...] = lax.dot_general(normed, wa.astype(jnp.bfloat16), (((1,), (1,)), ((), ())),
                              preferred_element_type=jnp.float32) + a_bias[0:1]
    group = iota((16, 128), 1) // 32
    for g in range(8):
        part = [pa[pl.ds(4 * g + k, 16, stride=32), :] for k in range(4)]
        out = jnp.where(group < 2, jnp.where(group == 0, part[0], part[1]), jnp.where(group == 2, part[2], part[3]))
        spread = jnp.dot(weights, ones_where(row[:32] == 4 * g + lane // 32), preferred_element_type=jnp.float32)
        a_ref[g * 16:(g + 1) * 16, :] = (out * spread).astype(jnp.bfloat16)
    by_four = ones_where(iota((32, 128), 1) == (row[:32] % 4) * 8 + row[:32] // 4)
    a_plain = jnp.dot(weights, by_four, preferred_element_type=jnp.float32)
    a_ref[128:136, :] = (a_plain[:8] + pltpu.roll(a_plain[8:], 64, 1)).astype(jnp.bfloat16)


def project(x, mask, present, gain, bias, weight, proj_bias):
    vmem = pl.BlockSpec(memory_space=pltpu.VMEM)
    out = [jax.ShapeDtypeStruct((136, 128), jnp.bfloat16)] * 2
    given = (x, mask, present[None], gain[None], bias[None], weight.T, proj_bias[None])
    return pl.pallas_call(
        project_kernel,
        out_shape=out,
        in_specs=[pl.BlockSpec(memory_space=pl.ANY)] * 7,
        out_specs=[vmem, vmem],
        scratch_shapes=[pltpu.VMEM(g.shape, g.dtype) for g in given] + [
            pltpu.VMEM((512, 128), jnp.float32), pltpu.VMEM((128, 128), jnp.float32), pltpu.SemaphoreType.DMA((7,))],
        compiler_params=pltpu.CompilerParams(vmem_limit_bytes=56 * 1024 * 1024),
        cost_estimate=pl.CostEstimate(flops=4 * 10**7, bytes_accessed=2**19, transcendentals=0),
        name="project",
    )(*given)


def fan_kernel(a_ref, o_ref, held, sems):
    load = pltpu.make_async_copy(a_ref, held, sems.at[32])
    load.start()
    load.wait()
    copies = [pltpu.make_async_copy(held, o_ref.at[k], sems.at[k]) for k in range(32)]
    for copy in copies:
        copy.start()
    for copy in copies:
        copy.wait()


def fan(a):
    return pl.pallas_call(
        fan_kernel,
        out_shape=jax.ShapeDtypeStruct((32, 136, 128), jnp.bfloat16),
        in_specs=[pl.BlockSpec(memory_space=pl.ANY)],
        out_specs=pl.BlockSpec(memory_space=pl.ANY),
        scratch_shapes=[pltpu.VMEM((136, 128), jnp.bfloat16), pltpu.SemaphoreType.DMA((33,))],
        compiler_params=pltpu.CompilerParams(vmem_limit_bytes=56 * 1024 * 1024),
        cost_estimate=pl.CostEstimate(flops=10**9, bytes_accessed=2**21, transcendentals=0),
        name="fan",
    )(a)


def columns_kernel(b_ref, o_ref, wb_ref):
    for g in range(8):
        o_ref[:, g * 128:(g + 1) * 128] = b_ref[:, g * 16:(g + 1) * 16, :].reshape(256, 128)
    wb_ref[...] = b_ref[:, 128:136, :].astype(jnp.float32).reshape(128, 128).astype(jnp.bfloat16)


def columns(b_all):
    vmem = pl.BlockSpec(memory_space=pltpu.VMEM)
    return pl.pallas_call(
        columns_kernel,
        out_shape=[jax.ShapeDtypeStruct(shape, jnp.bfloat16) for shape in ((256, 1024), (128, 128))],
        in_specs=[vmem],
        out_specs=[vmem, vmem],
        compiler_params=pltpu.CompilerParams(vmem_limit_bytes=16 * 1024 * 1024),
        cost_estimate=pl.CostEstimate(flops=10**12, bytes_accessed=2**21, transcendentals=0),
        name="columns",
    )(b_all)


def tile(block, a_ref, b_ref, wb_ref, w_ref, bias_ref, at, xs, put):
    lane = iota((128, 128), 1)
    for g in range(8):
        at[g * 128:(g + 1) * 128, :] = a_ref[block, :, g * 16:(g + 1) * 16, :].reshape(256, 128).T
    wa = a_ref[block, :, 128:136, :].astype(jnp.float32).reshape(128, 128).astype(jnp.bfloat16)
    count = lax.dot_general(wa, wb_ref[...], (((0,), (0,)), ((), ())), preferred_element_type=jnp.float32)
    count = jnp.where(lane[:32] < 32, count[0:32] + pltpu.roll(count[64:96], 64, 1), 0.0)
    spread = count[0:8]
    for k in range(1, 4):
        spread += pltpu.roll(count[k * 8:(k + 1) * 8], 32 * k, 1)
    inv = 1.0 / jnp.maximum(spread, 1.0)
    bias = bias_ref[...]
    group = lane // 32
    for n in range(4):
        for m in range(4):
            o = jnp.dot(at[m * 256:(m + 1) * 256, :], b_ref[:, n * 256:(n + 1) * 256],
                        preferred_element_type=jnp.float32).astype(jnp.bfloat16)
            for k in range(8):
                i = m * 8 + k
                for t in range(2):
                    g = 2 * n + t
                    xs[i // 2, g * 32:(g + 1) * 32, (i % 2) * 128:(i % 2 + 1) * 128] = (
                        o[k * 32:(k + 1) * 32, t * 128:(t + 1) * 128])
    for q in range(8):
        y = [jnp.dot(w_ref[...], xs[2 * q + h], preferred_element_type=jnp.float32) for h in range(2)]
        part = [[y[i // 2][p * 128:(p + 1) * 128, (i % 2) * 128:(i % 2 + 1) * 128] for p in range(4)] for i in range(4)]
        z = bias
        for d in range(4):
            v = [part[(p + d) % 4][p] for p in range(4)]
            v = jnp.where(group < 2, jnp.where(group == 0, v[0], v[1]), jnp.where(group == 2, v[2], v[3]))
            z = z + (pltpu.roll(v, 32 * d, 1) if d else v)
        put(4 * q, (z * inv[q:q + 1]).T)


def foreign_kernel(xl_ref, a_ref, b_ref, wb_ref, w_ref, bias_ref, o_ref, at, xs):
    def put(i, z):
        o_ref[i:i + 4] = z.astype(jnp.bfloat16).reshape(4, 32, 128)

    tile(1 - xl_ref[0], a_ref, b_ref, wb_ref, w_ref, bias_ref, at, xs, put)


def own_kernel(xl_ref, a_ref, b_ref, wb_ref, w_ref, bias_ref, o_ref, at, xs, held, sem):
    def put(i, z):
        held[i:i + 4] = z.reshape(4, 32, 128)

    tile(xl_ref[0], a_ref, b_ref, wb_ref, w_ref, bias_ref, at, xs, put)
    copy = pltpu.make_async_copy(held, o_ref.at[:, pl.ds(pl.multiple_of(xl_ref[0] * 32, 32), 32), :], sem)
    copy.start()
    copy.wait()


def join_kernel(xl_ref, t_ref, given_ref, o_ref, held, sem):
    del given_ref
    held[...] = t_ref[...].astype(jnp.float32)
    copy = pltpu.make_async_copy(held, o_ref.at[:, pl.ds(pl.multiple_of((1 - xl_ref[0]) * 32, 32), 32), :], sem)
    copy.start()
    copy.wait()


def call(kernel, name, shape, dtype, out_space, scratch, flops, in_specs, aliases, args):
    return pl.pallas_call(
        kernel,
        out_shape=jax.ShapeDtypeStruct(shape, dtype),
        in_specs=in_specs,
        out_specs=pl.BlockSpec(memory_space=out_space),
        scratch_shapes=scratch,
        input_output_aliases=aliases,
        compiler_params=pltpu.CompilerParams(vmem_limit_bytes=24 * 1024 * 1024),
        cost_estimate=pl.CostEstimate(flops=flops, bytes_accessed=2**21, transcendentals=0),
        name=name,
    )(*args)


def shift(n, by):
    return [(i, (i + by) % n) for i in range(n)]


def local(x, mask, present, gain, bias, weight, proj_bias, out_weight, out_bias):
    a, b = project(x, mask, present, gain, bias, weight, proj_bias)
    turn = [((z * 2 + xl) * 16 + q, (q * 2 + xl) * 16 + z) for z in range(16) for xl in range(2) for q in range(16)]
    b = lax.ppermute(b, RES + SEQ, turn)
    w4 = out_weight.reshape(32, 8, 4, 128).transpose(2, 3, 1, 0).reshape(512, 256)
    a_all = lax.all_to_all(fan(a), ("xl",) + SEQ, 0, 0, tiled=True).reshape(2, 16, 136, 128)
    b_all = lax.all_gather(b, "z")
    b_all, wb = columns(b_all)
    a_all, b_all, wb = lax.optimization_barrier((a_all, b_all, wb))

    bias2 = jnp.broadcast_to(out_bias[:, None], (128, 128))
    xl = lax.axis_index("xl").astype(jnp.int32).reshape(1)
    smem, vmem, anywhere = (pl.BlockSpec(memory_space=m) for m in (pltpu.SMEM, pltpu.VMEM, pl.ANY))
    work = [pltpu.VMEM((1024, 256), jnp.bfloat16), pltpu.VMEM((16, 256, 256), jnp.bfloat16)]
    held = [pltpu.VMEM((32, 32, 128), jnp.float32), pltpu.SemaphoreType.DMA]
    args, specs = (xl, a_all, b_all, wb, w4, bias2), [smem] + [vmem] * 5
    sent = call(foreign_kernel, "foreign", (32, 32, 128), jnp.bfloat16, pltpu.VMEM, work, 10**9, specs, {}, args)
    taken = lax.ppermute(sent, "xl", shift(2, 1))
    out = call(own_kernel, "own", (32, 64, 128), jnp.float32, pl.ANY, work + held, 10**9, specs, {}, args)
    return call(join_kernel, "join", (32, 64, 128), jnp.float32, pl.ANY, held, 10**6, [smem, vmem, anywhere], {2: 0},
                (xl, taken, out))


def solution(mesh):
    fine = Mesh(mesh.devices.reshape(16, 2, 4, 2, 2), RES + SEQ)
    in_specs = (P(SEQ, RES, None), P(SEQ, RES), P(RES), P(), P(), P(), P(), P(), P())
    return jax.shard_map(local, mesh=fine, in_specs=in_specs, out_specs=P(RES, SEQ, None), check_vma=False)
```

```python
import jax
import jax.numpy as jnp
from jax import lax
from jax.experimental import pallas as pl
from jax.experimental.pallas import tpu as pltpu
from jax.sharding import Mesh, PartitionSpec as P

EPSILON = 1e-05
RES = ("z", "xl")
SEQ = ("y", "xh", "core")


def iota(shape, dim):
    return lax.broadcasted_iota(jnp.int32, shape, dim)


def ones_where(condition, dtype=jnp.bfloat16):
    return jnp.where(condition, 1.0, 0.0).astype(dtype)


def project_kernel(*refs):
    sources, (copies_ref, b_ref, tile_ref), held, (pa, tiles, a_ref, sems) = refs[:8], refs[8:11], refs[11:19], refs[19:]
    small = [pltpu.make_async_copy(src, dst, sems.at[k]) for k, (src, dst) in enumerate(zip(sources[1:], held[1:]))]
    large = pltpu.make_async_copy(sources[0], held[0], sems.at[7])
    for load in [large] + small:
        load.start()
    x_ref, mask_ref, present_ref, gain_ref, bias_ref, w_ref, pb_ref, ob_ref = held
    for load in small:
        load.wait()
    weights = (mask_ref[...] * present_ref[...]).astype(jnp.float32).astype(jnp.bfloat16)
    proj_w = w_ref[...]

    row, col = iota((32, 64), 0), iota((32, 64), 1)
    pick = ones_where(col == 32 + 4 * (row % 8) + row // 8)
    wb = jnp.dot(pick, proj_w, preferred_element_type=jnp.float32).astype(jnp.bfloat16)
    row, col = iota((8, 64), 0), iota((8, 64), 1)
    own = jnp.where((col >= 32) & ((col - 32) // 4 == row), pb_ref[...], 0.0)
    row, lane = iota((64, 128), 0), iota((64, 128), 1) // 32
    spread = ones_where(row % 4 == lane, jnp.float32)
    b_bias = jnp.dot(own, spread, precision=lax.Precision.HIGHEST, preferred_element_type=jnp.float32)
    four = ones_where(row == iota((64, 128), 1) % 32)
    wa = lax.dot_general(four, proj_w, (((0,), (0,)), ((), ())), preferred_element_type=jnp.float32)
    wa = wa.astype(jnp.bfloat16)
    a_bias = jnp.dot(jnp.broadcast_to(pb_ref[...], (8, 64)), four.astype(jnp.float32),
                     precision=lax.Precision.HIGHEST, preferred_element_type=jnp.float32)
    tile_ref[...] = jnp.broadcast_to(ob_ref[...], (128, 128)).T

    large.wait()
    value = x_ref[...].reshape(512, 256).astype(jnp.float32)
    mean = jnp.mean(value, axis=-1, keepdims=True)
    centred = value - mean
    var = jnp.mean(centred * centred, axis=-1, keepdims=True)
    normed = (centred * lax.rsqrt(var + EPSILON) * gain_ref[...] + bias_ref[...]).astype(jnp.bfloat16)
    pa[...] = lax.dot_general(normed, wa, (((1,), (1,)), ((), ())), preferred_element_type=jnp.float32) + a_bias[0:1]
    row, lane128 = iota((32, 128), 0), iota((32, 128), 1)
    group = iota((16, 128), 1) // 32
    for g in range(8):
        part = [pa[pl.ds(4 * g + k, 16, stride=32), :] for k in range(4)]
        out = jnp.where(group < 2, jnp.where(group == 0, part[0], part[1]), jnp.where(group == 2, part[2], part[3]))
        spread = jnp.dot(weights, ones_where(row == 4 * g + lane128 // 32), preferred_element_type=jnp.float32)
        a_ref[0, g * 16:(g + 1) * 16, :] = (out * spread).astype(jnp.bfloat16)
    a_plain = jnp.dot(weights, ones_where(lane128 == (row % 4) * 8 + row // 4), preferred_element_type=jnp.float32)
    a_ref[0, 128:136, :] = (a_plain[:8] + pltpu.roll(a_plain[8:], 64, 1)).astype(jnp.bfloat16)
    for k in range(1, 4):
        a_ref[k] = a_ref[0]
    copies = [pltpu.make_async_copy(a_ref, copies_ref.at[pl.ds(4 * k, 4)], sems.at[8 + k]) for k in range(8)]
    for copy in copies:
        copy.start()

    bt = lax.dot_general(wb, normed, (((1,), (1,)), ((), ())), preferred_element_type=jnp.float32)
    group = iota((8, 128), 1) // 32
    for t in range(4):
        parts = [bt[p * 8:(p + 1) * 8, t * 128:(t + 1) * 128] for p in range(4)]
        for r in range(4):
            out = parts[r]
            for p in range(4):
                if p != r:
                    out = jnp.where(group == p, pltpu.roll(parts[p], (32 * (p - r)) % 128, 1), out)
            tiles[pl.ds(4 * t + r, 8, stride=16), :] = out + b_bias
    b_weights = jnp.dot(weights, ones_where(lane128 % 32 == row), preferred_element_type=jnp.float32)
    for g in range(8):
        b_ref[g * 16:(g + 1) * 16, :] = (tiles[g * 16:(g + 1) * 16, :] * b_weights).astype(jnp.bfloat16)
    b_plain = jnp.where(iota((16, 128), 1) < 32, b_weights, 0.0)
    b_ref[128:136, :] = (b_plain[:8] + pltpu.roll(b_plain[8:], 64, 1)).astype(jnp.bfloat16)
    for copy in copies:
        copy.wait()


def project(x, mask, present, gain, bias, weight, proj_bias, out_bias):
    vmem = pl.BlockSpec(memory_space=pltpu.VMEM)
    out = [jax.ShapeDtypeStruct((32, 136, 128), jnp.bfloat16), jax.ShapeDtypeStruct((136, 128), jnp.bfloat16),
           jax.ShapeDtypeStruct((128, 128), jnp.float32)]
    given = (x, mask, present[None], gain[None], bias[None], weight.T, proj_bias[None], out_bias[None])
    return pl.pallas_call(
        project_kernel,
        out_shape=out,
        in_specs=[pl.BlockSpec(memory_space=pl.ANY)] * 8,
        out_specs=[pl.BlockSpec(memory_space=pl.ANY), vmem, vmem],
        scratch_shapes=[pltpu.VMEM(g.shape, g.dtype) for g in given] + [
            pltpu.VMEM((512, 128), jnp.float32), pltpu.VMEM((128, 128), jnp.float32),
            pltpu.VMEM((4, 136, 128), jnp.bfloat16), pltpu.SemaphoreType.DMA((16,))],
        compiler_params=pltpu.CompilerParams(vmem_limit_bytes=56 * 1024 * 1024),
        cost_estimate=pl.CostEstimate(flops=4 * 10**7, bytes_accessed=2**19, transcendentals=0),
        name="project",
    )(*given)


OFFSETS = ((2, 1), (1, 1), (3, 1), (2, 0), (0, 1), (1, 0), (3, 0), (0, 0))
PACKED = sum((y * 2 + xh) << 3 * k for k, (y, xh) in enumerate(OFFSETS))


def source(line, z):
    dz = (z - line) & 15
    rank = 2 * jnp.minimum(dz, 16 - dz) - jnp.where((dz >= 1) & (dz <= 8), 1, 0)
    offset = (PACKED >> (3 * (rank >> 1))) & 7
    y = (line >> 2) + (offset >> 1)
    xh = (line >> 1) ^ offset
    return (y & 3) * 4 + (xh & 1) * 2 + (rank & 1)


def columns_kernel(line_ref, b_ref, tile_ref, o_ref, wb_ref, bias_ref, packed):
    for z in range(16):
        at = source(line_ref[0], jnp.int32(z))
        rows = pl.ds(pl.multiple_of(at * 16, 16), 16)
        for g in range(8):
            v = b_ref[z, g * 16:(g + 1) * 16, :]
            o_ref[0, rows, g * 128:(g + 1) * 128] = v
            o_ref[1, rows, g * 128:(g + 1) * 128] = pltpu.roll(v.astype(jnp.float32), 64, 1).astype(jnp.bfloat16)
        packed[pl.ds(pl.multiple_of(at * 8, 8), 8), :] = b_ref[z, 128:136, :].astype(jnp.float32)
    wb_ref[...] = packed[...].astype(jnp.bfloat16)
    bias_ref[...] = tile_ref[...]


def columns(line, b_all, bias):
    vmem = pl.BlockSpec(memory_space=pltpu.VMEM)
    return pl.pallas_call(
        columns_kernel,
        out_shape=[jax.ShapeDtypeStruct((2, 256, 1024), jnp.bfloat16), jax.ShapeDtypeStruct((128, 128), jnp.bfloat16),
                   jax.ShapeDtypeStruct((128, 128), jnp.float32)],
        in_specs=[pl.BlockSpec(memory_space=pltpu.SMEM), vmem, vmem],
        out_specs=[vmem] * 3,
        scratch_shapes=[pltpu.VMEM((128, 128), jnp.float32)],
        compiler_params=pltpu.CompilerParams(vmem_limit_bytes=16 * 1024 * 1024),
        cost_estimate=pl.CostEstimate(flops=3*10**10, bytes_accessed=2**21, transcendentals=0),
        name="columns",
    )(line, b_all, bias)


def tile(block, a_ref, b_ref, wb_ref, w_ref, bias_ref, at, xs, put):
    lane = iota((128, 128), 1)
    for g in range(8):
        t = a_ref[block, :, g * 16:(g + 1) * 16, :].reshape(256, 128).T
        for k in range(4):
            i = 4 * g + k
            row = (i % 2) * 512 + (i // 2) * 32
            at[row:row + 32, :] = t[k * 32:(k + 1) * 32, :]
    wa = a_ref[block, :, 128:136, :].astype(jnp.float32).reshape(128, 128).astype(jnp.bfloat16)
    count = lax.dot_general(wa, wb_ref[...], (((0,), (0,)), ((), ())), preferred_element_type=jnp.float32)
    count = jnp.where(lane[:32] < 32, count[0:32] + pltpu.roll(count[64:96], 64, 1), 0.0)
    spread = count[0:8]
    for k in range(1, 4):
        spread += pltpu.roll(count[k * 8:(k + 1) * 8], 32 * (0, 2, 1, 3)[k], 1)
    inv = 1.0 / jnp.maximum(spread, 1.0)
    bias = bias_ref[...]
    low = lane < 64
    even = (lane // 32) % 2 == 0
    for n in range(4):
        for m in range(2):
            o = [jnp.dot(at[h * 512 + m * 256:h * 512 + (m + 1) * 256, :], b_ref[h, :, n * 256:(n + 1) * 256],
                         preferred_element_type=jnp.float32) for h in range(2)]
            for k in range(8):
                pair = m * 8 + k
                for t in range(2):
                    g = 2 * n + t
                    o0, o1 = (v[k * 32:(k + 1) * 32, t * 128:(t + 1) * 128] for v in o)
                    at_lane = slice((pair % 2) * 128, (pair % 2 + 1) * 128)
                    xs[0, pair // 2, g * 32:(g + 1) * 32, at_lane] = jnp.where(low[:32], o0, o1).astype(jnp.bfloat16)
                    xs[1, pair // 2, g * 32:(g + 1) * 32, at_lane] = jnp.where(low[:32], o1, o0).astype(jnp.bfloat16)
    for q in range(8):
        y = [jnp.dot(w_ref[h * 256:(h + 1) * 256, :], xs[h, q], preferred_element_type=jnp.float32) for h in range(2)]
        z = []
        for k in range(2):
            s0, s1 = (jnp.where(even, v[:128, k * 128:(k + 1) * 128], v[128:, k * 128:(k + 1) * 128]) for v in y)
            r = s0 + pltpu.roll(s1, 64, 1)
            z.append(r + pltpu.roll(r, 32 if k else 96, 1))
        put(q, ((jnp.where(even, z[0], z[1]) + bias) * inv[q:q + 1]).T)


def foreign_kernel(xl_ref, a_ref, b_ref, wb_ref, w_ref, bias_ref, o_ref, at, xs):
    def put(q, z):
        for k in range(4):
            o_ref[4 * q + (0, 2, 1, 3)[k]] = z[k * 32:(k + 1) * 32].astype(jnp.bfloat16)

    tile(1 - xl_ref[0], a_ref, b_ref, wb_ref, w_ref, bias_ref, at, xs, put)


def own_kernel(xl_ref, a_ref, b_ref, wb_ref, w_ref, bias_ref, o_ref, at, xs, held, sems):
    place = pl.ds(pl.multiple_of(xl_ref[0] * 32, 32), 32)
    copies = [pltpu.make_async_copy(held.at[pl.ds(4 * q, 4)], o_ref.at[pl.ds(4 * q, 4), place, :], sems.at[q])
              for q in range(8)]

    def put(q, z):
        for k in range(4):
            held[4 * q + (0, 2, 1, 3)[k]] = z[k * 32:(k + 1) * 32]
        copies[q].start()

    tile(xl_ref[0], a_ref, b_ref, wb_ref, w_ref, bias_ref, at, xs, put)
    for copy in copies:
        copy.wait()


def join_kernel(xl_ref, t_ref, given_ref, o_ref, held, sems):
    del given_ref
    place = pl.ds(pl.multiple_of((1 - xl_ref[0]) * 32, 32), 32)
    copies = [pltpu.make_async_copy(held.at[pl.ds(4 * q, 4)], o_ref.at[pl.ds(4 * q, 4), place, :], sems.at[q])
              for q in range(8)]
    for q in range(8):
        held[4 * q:4 * q + 4] = t_ref[4 * q:4 * q + 4].astype(jnp.float32)
        copies[q].start()
    for copy in copies:
        copy.wait()


def call(kernel, name, shape, dtype, out_space, scratch, flops, in_specs, aliases, args):
    return pl.pallas_call(
        kernel,
        out_shape=jax.ShapeDtypeStruct(shape, dtype),
        in_specs=in_specs,
        out_specs=pl.BlockSpec(memory_space=out_space),
        scratch_shapes=scratch,
        input_output_aliases=aliases,
        compiler_params=pltpu.CompilerParams(vmem_limit_bytes=24 * 1024 * 1024),
        cost_estimate=pl.CostEstimate(flops=flops, bytes_accessed=2**21, transcendentals=0),
        name=name,
    )(*args)


def shift(n, by):
    return [(i, (i + by) % n) for i in range(n)]


def places():
    out = []
    for line in range(16):
        row = []
        for z in range(16):
            dz = (z - line) % 16
            rank = 2 * min(dz, 16 - dz) - int(1 <= dz <= 8)
            y, xh = OFFSETS[rank // 2]
            row.append((line // 4 + y) % 4 * 4 + (line // 2 % 2 ^ xh) * 2 + rank % 2)
        out.append(row)
    return out


def local(x, mask, present, gain, bias, weight, proj_bias, out_weight, out_bias):
    a, b, bias2 = project(x, mask, present, gain, bias, weight, proj_bias, out_bias)
    turn = [((z * 2 + xl) * 16 + q, (at * 2 + xl) * 16 + z) for z, row in enumerate(places()) for xl in range(2)
            for at, q in enumerate(row)]
    b = lax.ppermute(b, RES + SEQ, turn)
    w4 = out_weight.reshape(32, 8, 4, 128).transpose(2, 3, 1, 0).reshape(512, 256)
    a_all = lax.all_to_all(a, ("xl",) + SEQ, 0, 0, tiled=True).reshape(2, 16, 136, 128)
    b_all = lax.all_gather(b, "z")
    line = sum(lax.axis_index(n) * k for n, k in zip(SEQ, (4, 2, 1))).astype(jnp.int32).reshape(1)
    b_all, wb, bias2 = columns(line, b_all, bias2)
    a_all, b_all = lax.optimization_barrier((a_all, b_all))

    xl = lax.axis_index("xl").astype(jnp.int32).reshape(1)
    smem, vmem, anywhere = (pl.BlockSpec(memory_space=m) for m in (pltpu.SMEM, pltpu.VMEM, pl.ANY))
    work = [pltpu.VMEM((1024, 256), jnp.bfloat16), pltpu.VMEM((2, 8, 256, 256), jnp.bfloat16)]
    held = [pltpu.VMEM((32, 32, 128), jnp.float32), pltpu.SemaphoreType.DMA((8,))]
    args, specs = (xl, a_all, b_all, wb, w4, bias2), [smem] + [vmem] * 5
    sent = call(foreign_kernel, "foreign", (32, 32, 128), jnp.bfloat16, pltpu.VMEM, work, 10**9, specs, {}, args)
    taken = lax.ppermute(sent, "xl", shift(2, 1))
    out = call(own_kernel, "own", (32, 64, 128), jnp.float32, pl.ANY, work + held, 10**9, specs, {}, args)
    return call(join_kernel, "join", (32, 64, 128), jnp.float32, pl.ANY, held, 10**6, [smem, vmem, anywhere], {2: 0},
                (xl, taken, out))


def solution(mesh):
    fine = Mesh(mesh.devices.reshape(16, 2, 4, 2, 2), RES + SEQ)
    in_specs = (P(SEQ, RES, None), P(SEQ, RES), P(RES), P(), P(), P(), P(), P(), P())
    return jax.shard_map(local, mesh=fine, in_specs=in_specs, out_specs=P(RES, SEQ, None), check_vma=False)
```

```python
import jax
import jax.numpy as jnp
from jax import lax
from jax.experimental import pallas as pl
from jax.experimental.pallas import tpu as pltpu
from jax.sharding import Mesh, PartitionSpec as P

EPSILON = 1e-05
RES = ("z", "xl")
SEQ = ("y", "xh", "core")


def iota(shape, dim):
    return lax.broadcasted_iota(jnp.int32, shape, dim)


def ones_where(condition, dtype=jnp.bfloat16):
    return jnp.where(condition, 1.0, 0.0).astype(dtype)


def project_kernel(*refs):
    sources, (copies_ref, b_ref, tile_ref, w4_ref), held, (pa, tiles, a_ref, wf, sems) = refs[:9], refs[9:13], refs[13:22], refs[22:]
    small = [pltpu.make_async_copy(src, dst, sems.at[k]) for k, (src, dst) in enumerate(zip(sources[1:8], held[1:8]))]
    last = pltpu.make_async_copy(sources[8], held[8], sems.at[16])
    large = pltpu.make_async_copy(sources[0], held[0], sems.at[7])
    for load in [large] + small + [last]:
        load.start()
    x_ref, mask_ref, present_ref, gain_ref, bias_ref, w_ref, pb_ref, ob_ref, ow_ref = held
    for load in small:
        load.wait()
    large.wait()
    weights = (mask_ref[...] * present_ref[...]).astype(jnp.float32).astype(jnp.bfloat16)
    proj_w = w_ref[...]

    row, col = iota((32, 64), 0), iota((32, 64), 1)
    pick = ones_where(col == 32 + 4 * (row % 8) + row // 8)
    wb = jnp.dot(pick, proj_w, preferred_element_type=jnp.float32).astype(jnp.bfloat16)
    row, col = iota((8, 64), 0), iota((8, 64), 1)
    own = jnp.where((col >= 32) & ((col - 32) // 4 == row), pb_ref[...], 0.0)
    row, lane = iota((64, 128), 0), iota((64, 128), 1) // 32
    spread = ones_where(row % 4 == lane, jnp.float32)
    b_bias = jnp.dot(own, spread, precision=lax.Precision.HIGHEST, preferred_element_type=jnp.float32)
    four = ones_where(row == iota((64, 128), 1) % 32)
    wa = lax.dot_general(four, proj_w, (((0,), (0,)), ((), ())), preferred_element_type=jnp.float32)
    wa = wa.astype(jnp.bfloat16)
    a_bias = jnp.dot(jnp.broadcast_to(pb_ref[...], (8, 64)), four.astype(jnp.float32),
                     precision=lax.Precision.HIGHEST, preferred_element_type=jnp.float32)
    tile_ref[...] = jnp.broadcast_to(ob_ref[...], (128, 128)).T

    value = x_ref[...].reshape(512, 256).astype(jnp.float32)
    mean = jnp.mean(value, axis=-1, keepdims=True)
    centred = value - mean
    var = jnp.mean(centred * centred, axis=-1, keepdims=True)
    normed = (centred * lax.rsqrt(var + EPSILON) * gain_ref[...] + bias_ref[...]).astype(jnp.bfloat16)
    pa[...] = lax.dot_general(normed, wa, (((1,), (1,)), ((), ())), preferred_element_type=jnp.float32) + a_bias[0:1]
    row, lane128 = iota((32, 128), 0), iota((32, 128), 1)
    group = iota((16, 128), 1) // 32
    for g in range(8):
        part = [pa[pl.ds(4 * g + k, 16, stride=32), :] for k in range(4)]
        out = jnp.where(group < 2, jnp.where(group == 0, part[0], part[1]), jnp.where(group == 2, part[2], part[3]))
        spread = jnp.dot(weights, ones_where(row == 4 * g + lane128 // 32), preferred_element_type=jnp.float32)
        a_ref[0, g * 16:(g + 1) * 16, :] = (out * spread).astype(jnp.bfloat16)
    a_plain = jnp.dot(weights, ones_where(lane128 == (row % 4) * 8 + row // 4), preferred_element_type=jnp.float32)
    a_ref[0, 128:136, :] = (a_plain[:8] + pltpu.roll(a_plain[8:], 64, 1)).astype(jnp.bfloat16)
    for k in range(1, 4):
        a_ref[k] = a_ref[0]
    copies = [pltpu.make_async_copy(a_ref, copies_ref.at[pl.ds(4 * k, 4)], sems.at[8 + k]) for k in range(8)]
    for copy in copies:
        copy.start()

    bt = lax.dot_general(wb, normed, (((1,), (1,)), ((), ())), preferred_element_type=jnp.float32)
    group = iota((8, 128), 1) // 32
    for t in range(4):
        parts = [bt[p * 8:(p + 1) * 8, t * 128:(t + 1) * 128] for p in range(4)]
        for r in range(4):
            out = parts[r]
            for p in range(4):
                if p != r:
                    out = jnp.where(group == p, pltpu.roll(parts[p], (32 * (p - r)) % 128, 1), out)
            tiles[pl.ds(4 * t + r, 8, stride=16), :] = out + b_bias
    b_weights = jnp.dot(weights, ones_where(lane128 % 32 == row), preferred_element_type=jnp.float32)
    for g in range(8):
        b_ref[g * 16:(g + 1) * 16, :] = (tiles[g * 16:(g + 1) * 16, :] * b_weights).astype(jnp.bfloat16)
    b_plain = jnp.where(iota((16, 128), 1) < 32, b_weights, 0.0)
    b_ref[128:136, :] = (b_plain[:8] + pltpu.roll(b_plain[8:], 64, 1)).astype(jnp.bfloat16)
    last.wait()
    wf[...] = ow_ref[...].astype(jnp.float32)
    for p in range(4):
        rows = jnp.concatenate([wf[pl.ds(4 * g + p, 32, stride=32), :] for g in range(8)], axis=0)
        w4_ref[p * 128:(p + 1) * 128, :] = rows.T.astype(jnp.bfloat16)
    for copy in copies:
        copy.wait()


def project(x, mask, present, gain, bias, weight, proj_bias, out_bias, out_weight):
    vmem = pl.BlockSpec(memory_space=pltpu.VMEM)
    out = [jax.ShapeDtypeStruct((32, 136, 128), jnp.bfloat16), jax.ShapeDtypeStruct((136, 128), jnp.bfloat16),
           jax.ShapeDtypeStruct((128, 128), jnp.float32), jax.ShapeDtypeStruct((512, 256), jnp.bfloat16)]
    given = (x, mask, present[None], gain[None], bias[None], weight.T, proj_bias[None], out_bias[None], out_weight)
    return pl.pallas_call(
        project_kernel,
        out_shape=out,
        in_specs=[pl.BlockSpec(memory_space=pl.ANY)] * 9,
        out_specs=[pl.BlockSpec(memory_space=pl.ANY), vmem, vmem, vmem],
        scratch_shapes=[pltpu.VMEM(g.shape, g.dtype) for g in given] + [
            pltpu.VMEM((512, 128), jnp.float32), pltpu.VMEM((128, 128), jnp.float32),
            pltpu.VMEM((4, 136, 128), jnp.bfloat16), pltpu.VMEM((1024, 128), jnp.float32), pltpu.SemaphoreType.DMA((17,))],
        compiler_params=pltpu.CompilerParams(vmem_limit_bytes=56 * 1024 * 1024),
        cost_estimate=pl.CostEstimate(flops=4 * 10**7, bytes_accessed=2**19, transcendentals=0),
        name="project",
    )(*given)


OFFSETS = ((2, 1), (1, 1), (3, 1), (2, 0), (0, 1), (1, 0), (3, 0), (0, 0))
PACKED = sum((y * 2 + xh) << 3 * k for k, (y, xh) in enumerate(OFFSETS))


def source(line, z):
    dz = (z - line) & 15
    rank = 2 * jnp.minimum(dz, 16 - dz) - jnp.where((dz >= 1) & (dz <= 8), 1, 0)
    offset = (PACKED >> (3 * (rank >> 1))) & 7
    y = (line >> 2) + (offset >> 1)
    xh = (line >> 1) ^ offset
    return (y & 3) * 4 + (xh & 1) * 2 + (rank & 1)


def columns_kernel(line_ref, b_ref, tile_ref, w_ref, o_ref, wb_ref, bias_ref, w4_ref, packed):
    for z in range(16):
        at = source(line_ref[0], jnp.int32(z))
        rows = pl.ds(pl.multiple_of(at * 16, 16), 16)
        for g in range(8):
            v = b_ref[z, g * 16:(g + 1) * 16, :]
            o_ref[0, rows, g * 128:(g + 1) * 128] = v
            o_ref[1, rows, g * 128:(g + 1) * 128] = pltpu.roll(v.astype(jnp.float32), 64, 1).astype(jnp.bfloat16)
        packed[pl.ds(pl.multiple_of(at * 8, 8), 8), :] = b_ref[z, 128:136, :].astype(jnp.float32)
    wb_ref[...] = packed[...].astype(jnp.bfloat16)
    bias_ref[...] = tile_ref[...]
    w4_ref[...] = w_ref[...]


def columns(line, b_all, bias, w4):
    vmem = pl.BlockSpec(memory_space=pltpu.VMEM)
    return pl.pallas_call(
        columns_kernel,
        out_shape=[jax.ShapeDtypeStruct((2, 256, 1024), jnp.bfloat16), jax.ShapeDtypeStruct((128, 128), jnp.bfloat16),
                   jax.ShapeDtypeStruct((128, 128), jnp.float32), jax.ShapeDtypeStruct((512, 256), jnp.bfloat16)],
        in_specs=[pl.BlockSpec(memory_space=pltpu.SMEM), vmem, vmem, vmem],
        out_specs=[vmem] * 4,
        scratch_shapes=[pltpu.VMEM((128, 128), jnp.float32)],
        compiler_params=pltpu.CompilerParams(vmem_limit_bytes=16 * 1024 * 1024),
        cost_estimate=pl.CostEstimate(flops=3*10**10, bytes_accessed=2**21, transcendentals=0),
        name="columns",
    )(line, b_all, bias, w4)


def tile(block, a_ref, b_ref, wb_ref, w_ref, bias_ref, at, xs, put):
    lane = iota((128, 128), 1)
    for g in range(8):
        t = a_ref[block, :, g * 16:(g + 1) * 16, :].reshape(256, 128).T
        for k in range(4):
            i = 4 * g + k
            row = (i % 2) * 512 + (i // 2) * 32
            at[row:row + 32, :] = t[k * 32:(k + 1) * 32, :]
    wa = a_ref[block, :, 128:136, :].astype(jnp.float32).reshape(128, 128).astype(jnp.bfloat16)
    count = lax.dot_general(wa, wb_ref[...], (((0,), (0,)), ((), ())), preferred_element_type=jnp.float32)
    count = jnp.where(lane[:32] < 32, count[0:32] + pltpu.roll(count[64:96], 64, 1), 0.0)
    spread = count[0:8]
    for k in range(1, 4):
        spread += pltpu.roll(count[k * 8:(k + 1) * 8], 32 * (0, 2, 1, 3)[k], 1)
    inv = 1.0 / jnp.maximum(spread, 1.0)
    bias = bias_ref[...]
    low = lane < 64
    even = (lane // 32) % 2 == 0
    for n in range(4):
        for m in range(2):
            o = [jnp.dot(at[h * 512 + m * 256:h * 512 + (m + 1) * 256, :], b_ref[h, :, n * 256:(n + 1) * 256],
                         preferred_element_type=jnp.float32) for h in range(2)]
            for k in range(8):
                pair = m * 8 + k
                for t in range(2):
                    g = 2 * n + t
                    o0, o1 = (v[k * 32:(k + 1) * 32, t * 128:(t + 1) * 128] for v in o)
                    at_lane = slice((pair % 2) * 128, (pair % 2 + 1) * 128)
                    xs[0, pair // 2, g * 32:(g + 1) * 32, at_lane] = jnp.where(low[:32], o0, o1).astype(jnp.bfloat16)
                    xs[1, pair // 2, g * 32:(g + 1) * 32, at_lane] = jnp.where(low[:32], o1, o0).astype(jnp.bfloat16)
    for q in range(8):
        y = [jnp.dot(w_ref[h * 256:(h + 1) * 256, :], xs[h, q], preferred_element_type=jnp.float32) for h in range(2)]
        z = []
        for k in range(2):
            s0, s1 = (jnp.where(even, v[:128, k * 128:(k + 1) * 128], v[128:, k * 128:(k + 1) * 128]) for v in y)
            r = s0 + pltpu.roll(s1, 64, 1)
            z.append(r + pltpu.roll(r, 32 if k else 96, 1))
        put(q, ((jnp.where(even, z[0], z[1]) + bias) * inv[q:q + 1]).T)


def foreign_kernel(xl_ref, a_ref, b_ref, wb_ref, w_ref, bias_ref, o_ref, at, xs):
    def put(q, z):
        for k in range(4):
            o_ref[4 * q + (0, 2, 1, 3)[k]] = z[k * 32:(k + 1) * 32].astype(jnp.bfloat16)

    tile(1 - xl_ref[0], a_ref, b_ref, wb_ref, w_ref, bias_ref, at, xs, put)


def own_kernel(xl_ref, a_ref, b_ref, wb_ref, w_ref, bias_ref, o_ref, at, xs, held, sems):
    place = pl.ds(pl.multiple_of(xl_ref[0] * 32, 32), 32)
    copies = [pltpu.make_async_copy(held.at[pl.ds(4 * q, 4)], o_ref.at[pl.ds(4 * q, 4), place, :], sems.at[q])
              for q in range(8)]

    def put(q, z):
        for k in range(4):
            held[4 * q + (0, 2, 1, 3)[k]] = z[k * 32:(k + 1) * 32]
        copies[q].start()

    tile(xl_ref[0], a_ref, b_ref, wb_ref, w_ref, bias_ref, at, xs, put)
    for copy in copies:
        copy.wait()


def join_kernel(xl_ref, t_ref, given_ref, o_ref, held, sems):
    del given_ref
    place = pl.ds(pl.multiple_of((1 - xl_ref[0]) * 32, 32), 32)
    copies = [pltpu.make_async_copy(held.at[pl.ds(4 * q, 4)], o_ref.at[pl.ds(4 * q, 4), place, :], sems.at[q])
              for q in range(8)]
    for q in range(8):
        held[4 * q:4 * q + 4] = t_ref[4 * q:4 * q + 4].astype(jnp.float32)
        copies[q].start()
    for copy in copies:
        copy.wait()


def call(kernel, name, shape, dtype, out_space, scratch, flops, in_specs, aliases, args):
    return pl.pallas_call(
        kernel,
        out_shape=jax.ShapeDtypeStruct(shape, dtype),
        in_specs=in_specs,
        out_specs=pl.BlockSpec(memory_space=out_space),
        scratch_shapes=scratch,
        input_output_aliases=aliases,
        compiler_params=pltpu.CompilerParams(vmem_limit_bytes=24 * 1024 * 1024),
        cost_estimate=pl.CostEstimate(flops=flops, bytes_accessed=2**21, transcendentals=0),
        name=name,
    )(*args)


def shift(n, by):
    return [(i, (i + by) % n) for i in range(n)]


def places():
    out = []
    for line in range(16):
        row = []
        for z in range(16):
            dz = (z - line) % 16
            rank = 2 * min(dz, 16 - dz) - int(1 <= dz <= 8)
            y, xh = OFFSETS[rank // 2]
            row.append((line // 4 + y) % 4 * 4 + (line // 2 % 2 ^ xh) * 2 + rank % 2)
        out.append(row)
    return out


def local(x, mask, present, gain, bias, weight, proj_bias, out_weight, out_bias):
    a, b, bias2, w4 = project(x, mask, present, gain, bias, weight, proj_bias, out_bias, out_weight)
    turn = [((z * 2 + xl) * 16 + q, (at * 2 + xl) * 16 + z) for z, row in enumerate(places()) for xl in range(2)
            for at, q in enumerate(row)]
    b = lax.ppermute(b, RES + SEQ, turn)
    a_all = lax.all_to_all(a, ("xl",) + SEQ, 0, 0, tiled=True).reshape(2, 16, 136, 128)
    b_all = lax.all_gather(b, "z")
    line = sum(lax.axis_index(n) * k for n, k in zip(SEQ, (4, 2, 1))).astype(jnp.int32).reshape(1)
    b_all, wb, bias2, w4 = columns(line, b_all, bias2, w4)
    a_all, b_all = lax.optimization_barrier((a_all, b_all))

    xl = lax.axis_index("xl").astype(jnp.int32).reshape(1)
    smem, vmem, anywhere = (pl.BlockSpec(memory_space=m) for m in (pltpu.SMEM, pltpu.VMEM, pl.ANY))
    work = [pltpu.VMEM((1024, 256), jnp.bfloat16), pltpu.VMEM((2, 8, 256, 256), jnp.bfloat16)]
    held = [pltpu.VMEM((32, 32, 128), jnp.float32), pltpu.SemaphoreType.DMA((8,))]
    args, specs = (xl, a_all, b_all, wb, w4, bias2), [smem] + [vmem] * 5
    sent = call(foreign_kernel, "foreign", (32, 32, 128), jnp.bfloat16, pltpu.VMEM, work, 10**9, specs, {}, args)
    taken = lax.ppermute(sent, "xl", shift(2, 1))
    out = call(own_kernel, "own", (32, 64, 128), jnp.float32, pl.ANY, work + held, 10**9, specs, {}, args)
    return call(join_kernel, "join", (32, 64, 128), jnp.float32, pl.ANY, held, 10**6, [smem, vmem, anywhere], {2: 0},
                (xl, taken, out))


def solution(mesh):
    fine = Mesh(mesh.devices.reshape(16, 2, 4, 2, 2), RES + SEQ)
    in_specs = (P(SEQ, RES, None), P(SEQ, RES), P(RES), P(), P(), P(), P(), P(), P())
    return jax.shard_map(local, mesh=fine, in_specs=in_specs, out_specs=P(RES, SEQ, None), check_vma=False)
```

```python
import jax
import jax.numpy as jnp
from jax import lax
from jax.experimental import pallas as pl
from jax.experimental.pallas import tpu as pltpu
from jax.sharding import Mesh, PartitionSpec as P

EPSILON = 1e-05
RES = ("z", "xl")
SEQ = ("y", "xh", "core")


def iota(shape, dim):
    return lax.broadcasted_iota(jnp.int32, shape, dim)


def ones_where(condition, dtype=jnp.bfloat16):
    return jnp.where(condition, 1.0, 0.0).astype(dtype)


def project_kernel(*refs):
    sources, (copies_ref, b_ref, tile_ref, w4_ref), held, (pa, tiles, a_ref, wf, sems) = refs[:9], refs[9:13], refs[13:22], refs[22:]
    small = [pltpu.make_async_copy(src, dst, sems.at[k]) for k, (src, dst) in enumerate(zip(sources[1:8], held[1:8]))]
    last = pltpu.make_async_copy(sources[8], held[8], sems.at[16])
    large = pltpu.make_async_copy(sources[0], held[0], sems.at[7])
    for load in [large] + small + [last]:
        load.start()
    x_ref, mask_ref, present_ref, gain_ref, bias_ref, w_ref, pb_ref, ob_ref, ow_ref = held
    for load in small:
        load.wait()
    large.wait()
    weights = (mask_ref[...] * present_ref[...]).astype(jnp.float32).astype(jnp.bfloat16)
    proj_w = w_ref[...]

    row, col = iota((32, 64), 0), iota((32, 64), 1)
    pick = ones_where(col == 32 + 4 * (row % 8) + row // 8)
    wb = jnp.dot(pick, proj_w, preferred_element_type=jnp.float32).astype(jnp.bfloat16)
    row, col = iota((8, 64), 0), iota((8, 64), 1)
    own = jnp.where((col >= 32) & ((col - 32) // 4 == row), pb_ref[...], 0.0)
    row, lane = iota((64, 128), 0), iota((64, 128), 1) // 32
    spread = ones_where(row % 4 == lane, jnp.float32)
    b_bias = jnp.dot(own, spread, precision=lax.Precision.HIGHEST, preferred_element_type=jnp.float32)
    four = ones_where(row == iota((64, 128), 1) % 32)
    wa = lax.dot_general(four, proj_w, (((0,), (0,)), ((), ())), preferred_element_type=jnp.float32)
    wa = wa.astype(jnp.bfloat16)
    a_bias = jnp.dot(jnp.broadcast_to(pb_ref[...], (8, 64)), four.astype(jnp.float32),
                     precision=lax.Precision.HIGHEST, preferred_element_type=jnp.float32)
    tile_ref[...] = jnp.broadcast_to(ob_ref[...], (128, 128)).T

    value = x_ref[...].reshape(512, 256).astype(jnp.float32)
    mean = jnp.mean(value, axis=-1, keepdims=True)
    centred = value - mean
    var = jnp.mean(centred * centred, axis=-1, keepdims=True)
    normed = (centred * lax.rsqrt(var + EPSILON) * gain_ref[...] + bias_ref[...]).astype(jnp.bfloat16)
    pa[...] = lax.dot_general(normed, wa, (((1,), (1,)), ((), ())), preferred_element_type=jnp.float32) + a_bias[0:1]
    row, lane128 = iota((32, 128), 0), iota((32, 128), 1)
    group = iota((16, 128), 1) // 32
    for g in range(8):
        part = [pa[pl.ds(4 * g + k, 16, stride=32), :] for k in range(4)]
        out = jnp.where(group < 2, jnp.where(group == 0, part[0], part[1]), jnp.where(group == 2, part[2], part[3]))
        spread = jnp.dot(weights, ones_where(row == 4 * g + lane128 // 32), preferred_element_type=jnp.float32)
        a_ref[0, g * 16:(g + 1) * 16, :] = (out * spread).astype(jnp.bfloat16)
    a_plain = jnp.dot(weights, ones_where(lane128 == (row % 4) * 8 + row // 4), preferred_element_type=jnp.float32)
    a_ref[0, 128:144, :] = a_plain.astype(jnp.bfloat16)
    for k in range(1, 4):
        a_ref[k] = a_ref[0]
    copies = [pltpu.make_async_copy(a_ref, copies_ref.at[pl.ds(4 * k, 4)], sems.at[8 + k]) for k in range(8)]
    for copy in copies:
        copy.start()

    bt = lax.dot_general(wb, normed, (((1,), (1,)), ((), ())), preferred_element_type=jnp.float32)
    group = iota((8, 128), 1) // 32
    for t in range(4):
        parts = [bt[p * 8:(p + 1) * 8, t * 128:(t + 1) * 128] for p in range(4)]
        for r in range(4):
            out = parts[r]
            for p in range(4):
                if p != r:
                    out = jnp.where(group == p, pltpu.roll(parts[p], (32 * (p - r)) % 128, 1), out)
            tiles[pl.ds(4 * t + r, 8, stride=16), :] = out + b_bias
    b_weights = jnp.dot(weights, ones_where(lane128 % 32 == row), preferred_element_type=jnp.float32)
    for g in range(8):
        b_ref[g * 16:(g + 1) * 16, :] = (tiles[g * 16:(g + 1) * 16, :] * b_weights).astype(jnp.bfloat16)
    b_plain = jnp.where(iota((16, 128), 1) < 32, b_weights, 0.0)
    b_ref[128:144, :] = b_plain.astype(jnp.bfloat16)
    last.wait()
    wf[...] = ow_ref[...].astype(jnp.float32)
    for p in range(4):
        rows = jnp.concatenate([wf[pl.ds(4 * g + p, 32, stride=32), :] for g in range(8)], axis=0)
        w4_ref[p * 128:(p + 1) * 128, :] = rows.T.astype(jnp.bfloat16)
    for copy in copies:
        copy.wait()


def project(x, mask, present, gain, bias, weight, proj_bias, out_bias, out_weight):
    vmem = pl.BlockSpec(memory_space=pltpu.VMEM)
    out = [jax.ShapeDtypeStruct((32, 144, 128), jnp.bfloat16), jax.ShapeDtypeStruct((144, 128), jnp.bfloat16),
           jax.ShapeDtypeStruct((128, 128), jnp.float32), jax.ShapeDtypeStruct((512, 256), jnp.bfloat16)]
    given = (x, mask, present[None], gain[None], bias[None], weight.T, proj_bias[None], out_bias[None], out_weight)
    return pl.pallas_call(
        project_kernel,
        out_shape=out,
        in_specs=[pl.BlockSpec(memory_space=pl.ANY)] * 9,
        out_specs=[pl.BlockSpec(memory_space=pl.ANY), vmem, vmem, vmem],
        scratch_shapes=[pltpu.VMEM(g.shape, g.dtype) for g in given] + [
            pltpu.VMEM((512, 128), jnp.float32), pltpu.VMEM((128, 128), jnp.float32),
            pltpu.VMEM((4, 144, 128), jnp.bfloat16), pltpu.VMEM((1024, 128), jnp.float32), pltpu.SemaphoreType.DMA((17,))],
        compiler_params=pltpu.CompilerParams(vmem_limit_bytes=56 * 1024 * 1024),
        cost_estimate=pl.CostEstimate(flops=4 * 10**7, bytes_accessed=2**19, transcendentals=0),
        name="project",
    )(*given)


OFFSETS = ((2, 1), (1, 1), (3, 1), (2, 0), (0, 1), (1, 0), (3, 0), (0, 0))
PACKED = sum((y * 2 + xh) << 3 * k for k, (y, xh) in enumerate(OFFSETS))


def source(line, z):
    dz = (z - line) & 15
    rank = 2 * jnp.minimum(dz, 16 - dz) - jnp.where((dz >= 1) & (dz <= 8), 1, 0)
    offset = (PACKED >> (3 * (rank >> 1))) & 7
    y = (line >> 2) + (offset >> 1)
    xh = (line >> 1) ^ offset
    return (y & 3) * 4 + (xh & 1) * 2 + (rank & 1)


def columns_kernel(line_ref, b_ref, tile_ref, w_ref, o_ref, wb_ref, bias_ref, w4_ref):
    for z in range(16):
        at = source(line_ref[0], jnp.int32(z))
        rows = pl.ds(pl.multiple_of(at * 16, 16), 16)
        for g in range(8):
            v = b_ref[z, g * 16:(g + 1) * 16, :]
            o_ref[0, rows, g * 128:(g + 1) * 128] = v
            o_ref[1, rows, g * 128:(g + 1) * 128] = pltpu.roll(v.astype(jnp.float32), 64, 1).astype(jnp.bfloat16)
        wb_ref[rows, :] = b_ref[z, 128:144, :]
    bias_ref[...] = tile_ref[...]
    w4_ref[...] = w_ref[...]


def columns(line, b_all, bias, w4):
    vmem = pl.BlockSpec(memory_space=pltpu.VMEM)
    return pl.pallas_call(
        columns_kernel,
        out_shape=[jax.ShapeDtypeStruct((2, 256, 1024), jnp.bfloat16), jax.ShapeDtypeStruct((256, 128), jnp.bfloat16),
                   jax.ShapeDtypeStruct((128, 128), jnp.float32), jax.ShapeDtypeStruct((512, 256), jnp.bfloat16)],
        in_specs=[pl.BlockSpec(memory_space=pltpu.SMEM), vmem, vmem, vmem],
        out_specs=[vmem] * 4,
        compiler_params=pltpu.CompilerParams(vmem_limit_bytes=16 * 1024 * 1024),
        cost_estimate=pl.CostEstimate(flops=3*10**10, bytes_accessed=2**21, transcendentals=0),
        name="columns",
    )(line, b_all, bias, w4)


def tile(block, a_ref, b_ref, wb_ref, w_ref, bias_ref, at, xs, put):
    lane = iota((128, 128), 1)
    for g in range(8):
        t = a_ref[block, :, g * 16:(g + 1) * 16, :].reshape(256, 128).T
        for k in range(4):
            i = 4 * g + k
            row = (i % 2) * 512 + (i // 2) * 32
            at[row:row + 32, :] = t[k * 32:(k + 1) * 32, :]
    wa = a_ref[block, :, 128:144, :].reshape(256, 128)
    count = lax.dot_general(wa, wb_ref[...], (((0,), (0,)), ((), ())), preferred_element_type=jnp.float32)
    spread = count[0:8]
    for k in range(1, 4):
        spread += pltpu.roll(count[k * 8:(k + 1) * 8], 32 * (0, 2, 1, 3)[k], 1)
    inv = 1.0 / jnp.maximum(spread, 1.0)
    bias = bias_ref[...]
    low = lane < 64
    even = (lane // 32) % 2 == 0
    for n in range(4):
        for m in range(2):
            o = [jnp.dot(at[h * 512 + m * 256:h * 512 + (m + 1) * 256, :], b_ref[h, :, n * 256:(n + 1) * 256],
                         preferred_element_type=jnp.float32) for h in range(2)]
            for k in range(8):
                pair = m * 8 + k
                for t in range(2):
                    g = 2 * n + t
                    o0, o1 = (v[k * 32:(k + 1) * 32, t * 128:(t + 1) * 128] for v in o)
                    at_lane = slice((pair % 2) * 128, (pair % 2 + 1) * 128)
                    xs[0, pair // 2, g * 32:(g + 1) * 32, at_lane] = jnp.where(low[:32], o0, o1).astype(jnp.bfloat16)
                    xs[1, pair // 2, g * 32:(g + 1) * 32, at_lane] = jnp.where(low[:32], o1, o0).astype(jnp.bfloat16)
    for q in range(8):
        y = [jnp.dot(w_ref[h * 256:(h + 1) * 256, :], xs[h, q], preferred_element_type=jnp.float32) for h in range(2)]
        z = []
        for k in range(2):
            s0, s1 = (jnp.where(even, v[:128, k * 128:(k + 1) * 128], v[128:, k * 128:(k + 1) * 128]) for v in y)
            r = s0 + pltpu.roll(s1, 64, 1)
            z.append(r + pltpu.roll(r, 32 if k else 96, 1))
        put(q, ((jnp.where(even, z[0], z[1]) + bias) * inv[q:q + 1]).T)


def foreign_kernel(xl_ref, a_ref, b_ref, wb_ref, w_ref, bias_ref, o_ref, at, xs):
    def put(q, z):
        for k in range(4):
            o_ref[4 * q + (0, 2, 1, 3)[k]] = z[k * 32:(k + 1) * 32].astype(jnp.bfloat16)

    tile(1 - xl_ref[0], a_ref, b_ref, wb_ref, w_ref, bias_ref, at, xs, put)


def own_kernel(xl_ref, a_ref, b_ref, wb_ref, w_ref, bias_ref, o_ref, at, xs, held, sems):
    place = pl.ds(pl.multiple_of(xl_ref[0] * 32, 32), 32)
    copies = [pltpu.make_async_copy(held.at[pl.ds(4 * q, 4)], o_ref.at[pl.ds(4 * q, 4), place, :], sems.at[q])
              for q in range(8)]

    def put(q, z):
        for k in range(4):
            held[4 * q + (0, 2, 1, 3)[k]] = z[k * 32:(k + 1) * 32]
        copies[q].start()

    tile(xl_ref[0], a_ref, b_ref, wb_ref, w_ref, bias_ref, at, xs, put)
    for copy in copies:
        copy.wait()


def join_kernel(xl_ref, t_ref, given_ref, o_ref, held, sems):
    del given_ref
    place = pl.ds(pl.multiple_of((1 - xl_ref[0]) * 32, 32), 32)
    copies = [pltpu.make_async_copy(held.at[pl.ds(4 * q, 4)], o_ref.at[pl.ds(4 * q, 4), place, :], sems.at[q])
              for q in range(8)]
    for q in range(8):
        held[4 * q:4 * q + 4] = t_ref[4 * q:4 * q + 4].astype(jnp.float32)
        copies[q].start()
    for copy in copies:
        copy.wait()


def call(kernel, name, shape, dtype, out_space, scratch, flops, in_specs, aliases, args):
    return pl.pallas_call(
        kernel,
        out_shape=jax.ShapeDtypeStruct(shape, dtype),
        in_specs=in_specs,
        out_specs=pl.BlockSpec(memory_space=out_space),
        scratch_shapes=scratch,
        input_output_aliases=aliases,
        compiler_params=pltpu.CompilerParams(vmem_limit_bytes=24 * 1024 * 1024),
        cost_estimate=pl.CostEstimate(flops=flops, bytes_accessed=2**21, transcendentals=0),
        name=name,
    )(*args)


def shift(n, by):
    return [(i, (i + by) % n) for i in range(n)]


def places():
    out = []
    for line in range(16):
        row = []
        for z in range(16):
            dz = (z - line) % 16
            rank = 2 * min(dz, 16 - dz) - int(1 <= dz <= 8)
            y, xh = OFFSETS[rank // 2]
            row.append((line // 4 + y) % 4 * 4 + (line // 2 % 2 ^ xh) * 2 + rank % 2)
        out.append(row)
    return out


def local(x, mask, present, gain, bias, weight, proj_bias, out_weight, out_bias):
    a, b, bias2, w4 = project(x, mask, present, gain, bias, weight, proj_bias, out_bias, out_weight)
    turn = [((z * 2 + xl) * 16 + q, (at * 2 + xl) * 16 + z) for z, row in enumerate(places()) for xl in range(2)
            for at, q in enumerate(row)]
    b = lax.ppermute(b, RES + SEQ, turn)
    a_all = lax.all_to_all(a, ("xl",) + SEQ, 0, 0, tiled=True).reshape(2, 16, 144, 128)
    b_all = lax.all_gather(b, "z")
    line = sum(lax.axis_index(n) * k for n, k in zip(SEQ, (4, 2, 1))).astype(jnp.int32).reshape(1)
    b_all, wb, bias2, w4 = columns(line, b_all, bias2, w4)
    a_all, b_all = lax.optimization_barrier((a_all, b_all))

    xl = lax.axis_index("xl").astype(jnp.int32).reshape(1)
    smem, vmem, anywhere = (pl.BlockSpec(memory_space=m) for m in (pltpu.SMEM, pltpu.VMEM, pl.ANY))
    work = [pltpu.VMEM((1024, 256), jnp.bfloat16), pltpu.VMEM((2, 8, 256, 256), jnp.bfloat16)]
    held = [pltpu.VMEM((32, 32, 128), jnp.float32), pltpu.SemaphoreType.DMA((8,))]
    args, specs = (xl, a_all, b_all, wb, w4, bias2), [smem] + [vmem] * 5
    sent = call(foreign_kernel, "foreign", (32, 32, 128), jnp.bfloat16, pltpu.VMEM, work, 10**9, specs, {}, args)
    taken = lax.ppermute(sent, "xl", shift(2, 1))
    out = call(own_kernel, "own", (32, 64, 128), jnp.float32, pl.ANY, work + held, 10**9, specs, {}, args)
    return call(join_kernel, "join", (32, 64, 128), jnp.float32, pl.ANY, held, 10**6, [smem, vmem, anywhere], {2: 0},
                (xl, taken, out))


def solution(mesh):
    fine = Mesh(mesh.devices.reshape(16, 2, 4, 2, 2), RES + SEQ)
    in_specs = (P(SEQ, RES, None), P(SEQ, RES), P(RES), P(), P(), P(), P(), P(), P())
    return jax.shard_map(local, mesh=fine, in_specs=in_specs, out_specs=P(RES, SEQ, None), check_vma=False)
```

```python
import jax
import jax.numpy as jnp
from jax import lax
from jax.experimental import pallas as pl
from jax.experimental.pallas import tpu as pltpu
from jax.sharding import Mesh, PartitionSpec as P

EPSILON = 1e-05
RES = ("z", "xl")
SEQ = ("y", "xh", "core")


def iota(shape, dim):
    return lax.broadcasted_iota(jnp.int32, shape, dim)


def ones_where(condition, dtype=jnp.bfloat16):
    return jnp.where(condition, 1.0, 0.0).astype(dtype)


def project_kernel(*refs):
    sources, (copies_ref, *results), held, (pa, tiles, a_ref, wf, b_ref, tile_ref, w4_ref, sems) = (
        refs[:9], refs[9:13], refs[13:22], refs[22:])
    leave = [pltpu.make_async_copy(src, dst, sems.at[17 + k])
             for k, (src, dst) in enumerate(zip((b_ref, tile_ref, w4_ref), results))]
    small = [pltpu.make_async_copy(src, dst, sems.at[k]) for k, (src, dst) in enumerate(zip(sources[1:8], held[1:8]))]
    last = pltpu.make_async_copy(sources[8], held[8], sems.at[16])
    large = pltpu.make_async_copy(sources[0], held[0], sems.at[7])
    for load in [large] + small + [last]:
        load.start()
    x_ref, mask_ref, present_ref, gain_ref, bias_ref, w_ref, pb_ref, ob_ref, ow_ref = held
    for load in small:
        load.wait()
    large.wait()
    weights = (mask_ref[...] * present_ref[...]).astype(jnp.float32).astype(jnp.bfloat16)
    proj_w = w_ref[...]

    row, col = iota((32, 64), 0), iota((32, 64), 1)
    pick = ones_where(col == 32 + 4 * (row % 8) + row // 8)
    wb = jnp.dot(pick, proj_w, preferred_element_type=jnp.float32).astype(jnp.bfloat16)
    row, col = iota((8, 64), 0), iota((8, 64), 1)
    own = jnp.where((col >= 32) & ((col - 32) // 4 == row), pb_ref[...], 0.0)
    row, lane = iota((64, 128), 0), iota((64, 128), 1) // 32
    spread = ones_where(row % 4 == lane, jnp.float32)
    b_bias = jnp.dot(own, spread, precision=lax.Precision.HIGHEST, preferred_element_type=jnp.float32)
    four = ones_where(row == iota((64, 128), 1) % 32)
    wa = lax.dot_general(four, proj_w, (((0,), (0,)), ((), ())), preferred_element_type=jnp.float32)
    wa = wa.astype(jnp.bfloat16)
    a_bias = jnp.dot(jnp.broadcast_to(pb_ref[...], (8, 64)), four.astype(jnp.float32),
                     precision=lax.Precision.HIGHEST, preferred_element_type=jnp.float32)
    tile_ref[...] = jnp.broadcast_to(ob_ref[...], (128, 128)).T
    leave[1].start()

    value = x_ref[...].reshape(512, 256).astype(jnp.float32)
    mean = jnp.mean(value, axis=-1, keepdims=True)
    centred = value - mean
    var = jnp.mean(centred * centred, axis=-1, keepdims=True)
    normed = (centred * lax.rsqrt(var + EPSILON) * gain_ref[...] + bias_ref[...]).astype(jnp.bfloat16)
    pa[...] = lax.dot_general(normed, wa, (((1,), (1,)), ((), ())), preferred_element_type=jnp.float32) + a_bias[0:1]
    row, lane128 = iota((32, 128), 0), iota((32, 128), 1)
    group = iota((16, 128), 1) // 32
    for g in range(8):
        part = [pa[pl.ds(4 * g + k, 16, stride=32), :] for k in range(4)]
        out = jnp.where(group < 2, jnp.where(group == 0, part[0], part[1]), jnp.where(group == 2, part[2], part[3]))
        spread = jnp.dot(weights, ones_where(row == 4 * g + lane128 // 32), preferred_element_type=jnp.float32)
        a_ref[0, g * 16:(g + 1) * 16, :] = (out * spread).astype(jnp.bfloat16)
    a_plain = jnp.dot(weights, ones_where(lane128 == (row % 4) * 8 + row // 4), preferred_element_type=jnp.float32)
    a_ref[0, 128:144, :] = a_plain.astype(jnp.bfloat16)
    for k in range(1, 4):
        a_ref[k] = a_ref[0]
    copies = [pltpu.make_async_copy(a_ref, copies_ref.at[pl.ds(4 * k, 4)], sems.at[8 + k]) for k in range(8)]
    for copy in copies:
        copy.start()

    bt = lax.dot_general(wb, normed, (((1,), (1,)), ((), ())), preferred_element_type=jnp.float32)
    group = iota((8, 128), 1) // 32
    for t in range(4):
        parts = [bt[p * 8:(p + 1) * 8, t * 128:(t + 1) * 128] for p in range(4)]
        for r in range(4):
            out = parts[r]
            for p in range(4):
                if p != r:
                    out = jnp.where(group == p, pltpu.roll(parts[p], (32 * (p - r)) % 128, 1), out)
            tiles[pl.ds(4 * t + r, 8, stride=16), :] = out + b_bias
    b_weights = jnp.dot(weights, ones_where(lane128 % 32 == row), preferred_element_type=jnp.float32)
    for g in range(8):
        b_ref[g * 16:(g + 1) * 16, :] = (tiles[g * 16:(g + 1) * 16, :] * b_weights).astype(jnp.bfloat16)
    b_plain = jnp.where(iota((16, 128), 1) < 32, b_weights, 0.0)
    b_ref[128:144, :] = b_plain.astype(jnp.bfloat16)
    leave[0].start()
    last.wait()
    wf[...] = ow_ref[...].astype(jnp.float32)
    for p in range(4):
        rows = jnp.concatenate([wf[pl.ds(4 * g + p, 32, stride=32), :] for g in range(8)], axis=0)
        w4_ref[p * 128:(p + 1) * 128, :] = rows.T.astype(jnp.bfloat16)
    leave[2].start()
    for copy in copies + leave:
        copy.wait()


def project(x, mask, present, gain, bias, weight, proj_bias, out_bias, out_weight):
    out = [jax.ShapeDtypeStruct((32, 144, 128), jnp.bfloat16), jax.ShapeDtypeStruct((144, 128), jnp.bfloat16),
           jax.ShapeDtypeStruct((128, 128), jnp.float32), jax.ShapeDtypeStruct((512, 256), jnp.bfloat16)]
    given = (x, mask, present[None], gain[None], bias[None], weight.T, proj_bias[None], out_bias[None], out_weight)
    return pl.pallas_call(
        project_kernel,
        out_shape=out,
        in_specs=[pl.BlockSpec(memory_space=pl.ANY)] * 9,
        out_specs=[pl.BlockSpec(memory_space=pl.ANY)] * 4,
        scratch_shapes=[pltpu.VMEM(g.shape, g.dtype) for g in given] + [
            pltpu.VMEM((512, 128), jnp.float32), pltpu.VMEM((128, 128), jnp.float32),
            pltpu.VMEM((4, 144, 128), jnp.bfloat16), pltpu.VMEM((1024, 128), jnp.float32)] + [
            pltpu.VMEM(o.shape, o.dtype) for o in out[1:]] + [pltpu.SemaphoreType.DMA((20,))],
        compiler_params=pltpu.CompilerParams(vmem_limit_bytes=56 * 1024 * 1024),
        cost_estimate=pl.CostEstimate(flops=4 * 10**7, bytes_accessed=2**19, transcendentals=0),
        name="project",
    )(*given)


OFFSETS = ((2, 1), (1, 1), (3, 1), (2, 0), (0, 1), (1, 0), (3, 0), (0, 0))
PACKED = sum((y * 2 + xh) << 3 * k for k, (y, xh) in enumerate(OFFSETS))


def source(line, z):
    dz = (z - line) & 15
    rank = 2 * jnp.minimum(dz, 16 - dz) - jnp.where((dz >= 1) & (dz <= 8), 1, 0)
    offset = (PACKED >> (3 * (rank >> 1))) & 7
    y = (line >> 2) + (offset >> 1)
    xh = (line >> 1) ^ offset
    return (y & 3) * 4 + (xh & 1) * 2 + (rank & 1)


def columns_kernel(line_ref, b_ref, tile_ref, w_ref, o_ref, wb_ref, bias_ref, w4_ref):
    for z in range(16):
        at = source(line_ref[0], jnp.int32(z))
        rows = pl.ds(pl.multiple_of(at * 16, 16), 16)
        for g in range(8):
            v = b_ref[z, g * 16:(g + 1) * 16, :]
            o_ref[0, rows, g * 128:(g + 1) * 128] = v
            o_ref[1, rows, g * 128:(g + 1) * 128] = pltpu.roll(v.astype(jnp.float32), 64, 1).astype(jnp.bfloat16)
        wb_ref[rows, :] = b_ref[z, 128:144, :]
    bias_ref[...] = tile_ref[...]
    w4_ref[...] = w_ref[...]


def columns(line, b_all, bias, w4):
    vmem = pl.BlockSpec(memory_space=pltpu.VMEM)
    return pl.pallas_call(
        columns_kernel,
        out_shape=[jax.ShapeDtypeStruct((2, 256, 1024), jnp.bfloat16), jax.ShapeDtypeStruct((256, 128), jnp.bfloat16),
                   jax.ShapeDtypeStruct((128, 128), jnp.float32), jax.ShapeDtypeStruct((512, 256), jnp.bfloat16)],
        in_specs=[pl.BlockSpec(memory_space=pltpu.SMEM), vmem, vmem, vmem],
        out_specs=[vmem] * 4,
        compiler_params=pltpu.CompilerParams(vmem_limit_bytes=16 * 1024 * 1024),
        cost_estimate=pl.CostEstimate(flops=3*10**10, bytes_accessed=2**21, transcendentals=0),
        name="columns",
    )(line, b_all, bias, w4)


def tile(block, a_ref, b_ref, wb_ref, w_ref, bias_ref, at, xs, put):
    lane = iota((128, 128), 1)
    for g in range(8):
        t = a_ref[block, :, g * 16:(g + 1) * 16, :].reshape(256, 128).T
        for k in range(4):
            i = 4 * g + k
            row = (i % 2) * 512 + (i // 2) * 32
            at[row:row + 32, :] = t[k * 32:(k + 1) * 32, :]
    wa = a_ref[block, :, 128:144, :].reshape(256, 128)
    count = lax.dot_general(wa, wb_ref[...], (((0,), (0,)), ((), ())), preferred_element_type=jnp.float32)
    spread = count[0:8]
    for k in range(1, 4):
        spread += pltpu.roll(count[k * 8:(k + 1) * 8], 32 * (0, 2, 1, 3)[k], 1)
    inv = 1.0 / jnp.maximum(spread, 1.0)
    bias = bias_ref[...]
    low = lane < 64
    even = (lane // 32) % 2 == 0
    for n in range(4):
        for m in range(2):
            o = [jnp.dot(at[h * 512 + m * 256:h * 512 + (m + 1) * 256, :], b_ref[h, :, n * 256:(n + 1) * 256],
                         preferred_element_type=jnp.float32) for h in range(2)]
            for k in range(8):
                pair = m * 8 + k
                for t in range(2):
                    g = 2 * n + t
                    o0, o1 = (v[k * 32:(k + 1) * 32, t * 128:(t + 1) * 128] for v in o)
                    at_lane = slice((pair % 2) * 128, (pair % 2 + 1) * 128)
                    xs[0, pair // 2, g * 32:(g + 1) * 32, at_lane] = jnp.where(low[:32], o0, o1).astype(jnp.bfloat16)
                    xs[1, pair // 2, g * 32:(g + 1) * 32, at_lane] = jnp.where(low[:32], o1, o0).astype(jnp.bfloat16)
    for q in range(8):
        y = [jnp.dot(w_ref[h * 256:(h + 1) * 256, :], xs[h, q], preferred_element_type=jnp.float32) for h in range(2)]
        z = []
        for k in range(2):
            s0, s1 = (jnp.where(even, v[:128, k * 128:(k + 1) * 128], v[128:, k * 128:(k + 1) * 128]) for v in y)
            r = s0 + pltpu.roll(s1, 64, 1)
            z.append(r + pltpu.roll(r, 32 if k else 96, 1))
        put(q, ((jnp.where(even, z[0], z[1]) + bias) * inv[q:q + 1]).T)


def foreign_kernel(xl_ref, a_ref, b_ref, wb_ref, w_ref, bias_ref, o_ref, at, xs):
    def put(q, z):
        for k in range(4):
            o_ref[4 * q + (0, 2, 1, 3)[k]] = z[k * 32:(k + 1) * 32].astype(jnp.bfloat16)

    tile(1 - xl_ref[0], a_ref, b_ref, wb_ref, w_ref, bias_ref, at, xs, put)


def own_kernel(xl_ref, a_ref, b_ref, wb_ref, w_ref, bias_ref, o_ref, at, xs, held, sems):
    place = pl.ds(pl.multiple_of(xl_ref[0] * 32, 32), 32)
    copies = [pltpu.make_async_copy(held.at[pl.ds(4 * q, 4)], o_ref.at[pl.ds(4 * q, 4), place, :], sems.at[q])
              for q in range(8)]

    def put(q, z):
        for k in range(4):
            held[4 * q + (0, 2, 1, 3)[k]] = z[k * 32:(k + 1) * 32]
        copies[q].start()

    tile(xl_ref[0], a_ref, b_ref, wb_ref, w_ref, bias_ref, at, xs, put)
    for copy in copies:
        copy.wait()


def join_kernel(xl_ref, t_ref, given_ref, o_ref, held, sems):
    del given_ref
    place = pl.ds(pl.multiple_of((1 - xl_ref[0]) * 32, 32), 32)
    copies = [pltpu.make_async_copy(held.at[pl.ds(4 * q, 4)], o_ref.at[pl.ds(4 * q, 4), place, :], sems.at[q])
              for q in range(8)]
    for q in range(8):
        held[4 * q:4 * q + 4] = t_ref[4 * q:4 * q + 4].astype(jnp.float32)
        copies[q].start()
    for copy in copies:
        copy.wait()


def call(kernel, name, shape, dtype, out_space, scratch, flops, in_specs, aliases, args):
    return pl.pallas_call(
        kernel,
        out_shape=jax.ShapeDtypeStruct(shape, dtype),
        in_specs=in_specs,
        out_specs=pl.BlockSpec(memory_space=out_space),
        scratch_shapes=scratch,
        input_output_aliases=aliases,
        compiler_params=pltpu.CompilerParams(vmem_limit_bytes=24 * 1024 * 1024),
        cost_estimate=pl.CostEstimate(flops=flops, bytes_accessed=2**21, transcendentals=0),
        name=name,
    )(*args)


def shift(n, by):
    return [(i, (i + by) % n) for i in range(n)]


def places():
    out = []
    for line in range(16):
        row = []
        for z in range(16):
            dz = (z - line) % 16
            rank = 2 * min(dz, 16 - dz) - int(1 <= dz <= 8)
            y, xh = OFFSETS[rank // 2]
            row.append((line // 4 + y) % 4 * 4 + (line // 2 % 2 ^ xh) * 2 + rank % 2)
        out.append(row)
    return out


def local(x, mask, present, gain, bias, weight, proj_bias, out_weight, out_bias):
    a, b, bias2, w4 = project(x, mask, present, gain, bias, weight, proj_bias, out_bias, out_weight)
    turn = [((z * 2 + xl) * 16 + q, (at * 2 + xl) * 16 + z) for z, row in enumerate(places()) for xl in range(2)
            for at, q in enumerate(row)]
    b = lax.ppermute(b, RES + SEQ, turn)
    a_all = lax.all_to_all(a, ("xl",) + SEQ, 0, 0, tiled=True).reshape(2, 16, 144, 128)
    b_all = lax.all_gather(b, "z")
    line = sum(lax.axis_index(n) * k for n, k in zip(SEQ, (4, 2, 1))).astype(jnp.int32).reshape(1)
    b_all, wb, bias2, w4 = columns(line, b_all, bias2, w4)
    a_all, b_all = lax.optimization_barrier((a_all, b_all))

    xl = lax.axis_index("xl").astype(jnp.int32).reshape(1)
    smem, vmem, anywhere = (pl.BlockSpec(memory_space=m) for m in (pltpu.SMEM, pltpu.VMEM, pl.ANY))
    work = [pltpu.VMEM((1024, 256), jnp.bfloat16), pltpu.VMEM((2, 8, 256, 256), jnp.bfloat16)]
    held = [pltpu.VMEM((32, 32, 128), jnp.float32), pltpu.SemaphoreType.DMA((8,))]
    args, specs = (xl, a_all, b_all, wb, w4, bias2), [smem] + [vmem] * 5
    sent = call(foreign_kernel, "foreign", (32, 32, 128), jnp.bfloat16, pltpu.VMEM, work, 10**9, specs, {}, args)
    taken = lax.ppermute(sent, "xl", shift(2, 1))
    out = call(own_kernel, "own", (32, 64, 128), jnp.float32, pl.ANY, work + held, 10**9, specs, {}, args)
    return call(join_kernel, "join", (32, 64, 128), jnp.float32, pl.ANY, held, 10**6, [smem, vmem, anywhere], {2: 0},
                (xl, taken, out))


def solution(mesh):
    fine = Mesh(mesh.devices.reshape(16, 2, 4, 2, 2), RES + SEQ)
    in_specs = (P(SEQ, RES, None), P(SEQ, RES), P(RES), P(), P(), P(), P(), P(), P())
    return jax.shard_map(local, mesh=fine, in_specs=in_specs, out_specs=P(RES, SEQ, None), check_vma=False)
```

```python
import jax
import jax.numpy as jnp
from jax import lax
from jax.experimental import pallas as pl
from jax.experimental.pallas import tpu as pltpu
from jax.sharding import Mesh, PartitionSpec as P

EPSILON = 1e-05
RES = ("z", "xl")
SEQ = ("y", "xh", "core")


def iota(shape, dim):
    return lax.broadcasted_iota(jnp.int32, shape, dim)


def ones_where(condition, dtype=jnp.bfloat16):
    return jnp.where(condition, 1.0, 0.0).astype(dtype)


def project_kernel(*refs):
    sources, (copies_ref, *results), held, (pa, tiles, a_ref, wf, b_ref, tile_ref, w4_ref, sems) = (
        refs[:9], refs[9:13], refs[13:22], refs[22:])
    leave = [pltpu.make_async_copy(src, dst, sems.at[17 + k])
             for k, (src, dst) in enumerate(zip((b_ref, tile_ref, w4_ref), results))]
    small = [pltpu.make_async_copy(src, dst, sems.at[k]) for k, (src, dst) in enumerate(zip(sources[1:8], held[1:8]))]
    last = pltpu.make_async_copy(sources[8], held[8], sems.at[16])
    large = pltpu.make_async_copy(sources[0], held[0], sems.at[7])
    for load in [large] + small + [last]:
        load.start()
    x_ref, mask_ref, present_ref, gain_ref, bias_ref, w_ref, pb_ref, ob_ref, ow_ref = held
    for load in small:
        load.wait()
    large.wait()
    weights = (mask_ref[...] * present_ref[...]).astype(jnp.float32).astype(jnp.bfloat16)
    proj_w = w_ref[...]

    row, col = iota((32, 64), 0), iota((32, 64), 1)
    pick = ones_where(col == 32 + 4 * (row % 8) + row // 8)
    wb = jnp.dot(pick, proj_w, preferred_element_type=jnp.float32).astype(jnp.bfloat16)
    row, col = iota((8, 64), 0), iota((8, 64), 1)
    own = jnp.where((col >= 32) & ((col - 32) // 4 == row), pb_ref[...], 0.0)
    row, lane = iota((64, 128), 0), iota((64, 128), 1) // 32
    spread = ones_where(row % 4 == lane, jnp.float32)
    b_bias = jnp.dot(own, spread, precision=lax.Precision.HIGHEST, preferred_element_type=jnp.float32)
    four = ones_where(row == iota((64, 128), 1) % 32)
    wa = lax.dot_general(four, proj_w, (((0,), (0,)), ((), ())), preferred_element_type=jnp.float32)
    wa = wa.astype(jnp.bfloat16)
    a_bias = jnp.dot(jnp.broadcast_to(pb_ref[...], (8, 64)), four.astype(jnp.float32),
                     precision=lax.Precision.HIGHEST, preferred_element_type=jnp.float32)
    tile_ref[...] = jnp.broadcast_to(ob_ref[...], (128, 128)).T
    leave[1].start()

    value = x_ref[...].reshape(512, 256).astype(jnp.float32)
    mean = jnp.mean(value, axis=-1, keepdims=True)
    centred = value - mean
    var = jnp.mean(centred * centred, axis=-1, keepdims=True)
    normed = (centred * lax.rsqrt(var + EPSILON) * gain_ref[...] + bias_ref[...]).astype(jnp.bfloat16)
    pa[...] = lax.dot_general(normed, wa, (((1,), (1,)), ((), ())), preferred_element_type=jnp.float32) + a_bias[0:1]
    row, lane128 = iota((32, 128), 0), iota((32, 128), 1)
    group = iota((16, 128), 1) // 32
    for g in range(8):
        part = [pa[pl.ds(4 * g + k, 16, stride=32), :] for k in range(4)]
        out = jnp.where(group < 2, jnp.where(group == 0, part[0], part[1]), jnp.where(group == 2, part[2], part[3]))
        spread = jnp.dot(weights, ones_where(row == 4 * g + lane128 // 32), preferred_element_type=jnp.float32)
        a_ref[0, g * 16:(g + 1) * 16, :] = (out * spread).astype(jnp.bfloat16)
    a_plain = jnp.dot(weights, ones_where(lane128 == (row % 4) * 8 + row // 4), preferred_element_type=jnp.float32)
    a_ref[0, 128:144, :] = a_plain.astype(jnp.bfloat16)
    for k in range(1, 4):
        a_ref[k] = a_ref[0]
    copies = [pltpu.make_async_copy(a_ref, copies_ref.at[pl.ds(4 * k, 4)], sems.at[8 + k]) for k in range(8)]
    for copy in copies:
        copy.start()

    last.wait()
    wf[...] = ow_ref[...].astype(jnp.float32)
    for p in range(4):
        rows = jnp.concatenate([wf[pl.ds(4 * g + p, 32, stride=32), :] for g in range(8)], axis=0)
        w4_ref[p * 128:(p + 1) * 128, :] = rows.T.astype(jnp.bfloat16)
    leave[2].start()

    bt = lax.dot_general(wb, normed, (((1,), (1,)), ((), ())), preferred_element_type=jnp.float32)
    group = iota((8, 128), 1) // 32
    for t in range(4):
        parts = [bt[p * 8:(p + 1) * 8, t * 128:(t + 1) * 128] for p in range(4)]
        for r in range(4):
            out = parts[r]
            for p in range(4):
                if p != r:
                    out = jnp.where(group == p, pltpu.roll(parts[p], (32 * (p - r)) % 128, 1), out)
            tiles[pl.ds(4 * t + r, 8, stride=16), :] = out + b_bias
    b_weights = jnp.dot(weights, ones_where(lane128 % 32 == row), preferred_element_type=jnp.float32)
    for g in range(8):
        b_ref[g * 16:(g + 1) * 16, :] = (tiles[g * 16:(g + 1) * 16, :] * b_weights).astype(jnp.bfloat16)
    b_plain = jnp.where(iota((16, 128), 1) < 32, b_weights, 0.0)
    b_ref[128:144, :] = b_plain.astype(jnp.bfloat16)
    leave[0].start()
    for copy in copies + leave:
        copy.wait()


def project(x, mask, present, gain, bias, weight, proj_bias, out_bias, out_weight):
    out = [jax.ShapeDtypeStruct((32, 144, 128), jnp.bfloat16), jax.ShapeDtypeStruct((144, 128), jnp.bfloat16),
           jax.ShapeDtypeStruct((128, 128), jnp.float32), jax.ShapeDtypeStruct((512, 256), jnp.bfloat16)]
    given = (x, mask, present[None], gain[None], bias[None], weight.T, proj_bias[None], out_bias[None], out_weight)
    return pl.pallas_call(
        project_kernel,
        out_shape=out,
        in_specs=[pl.BlockSpec(memory_space=pl.ANY)] * 9,
        out_specs=[pl.BlockSpec(memory_space=pl.ANY)] * 4,
        scratch_shapes=[pltpu.VMEM(g.shape, g.dtype) for g in given] + [
            pltpu.VMEM((512, 128), jnp.float32), pltpu.VMEM((128, 128), jnp.float32),
            pltpu.VMEM((4, 144, 128), jnp.bfloat16), pltpu.VMEM((1024, 128), jnp.float32)] + [
            pltpu.VMEM(o.shape, o.dtype) for o in out[1:]] + [pltpu.SemaphoreType.DMA((20,))],
        compiler_params=pltpu.CompilerParams(vmem_limit_bytes=56 * 1024 * 1024),
        cost_estimate=pl.CostEstimate(flops=4 * 10**7, bytes_accessed=2**19, transcendentals=0),
        name="project",
    )(*given)


OFFSETS = ((2, 1), (1, 1), (3, 1), (2, 0), (0, 1), (1, 0), (3, 0), (0, 0))
PACKED = sum((y * 2 + xh) << 3 * k for k, (y, xh) in enumerate(OFFSETS))


def source(line, z):
    dz = (z - line) & 15
    rank = 2 * jnp.minimum(dz, 16 - dz) - jnp.where((dz >= 1) & (dz <= 8), 1, 0)
    offset = (PACKED >> (3 * (rank >> 1))) & 7
    y = (line >> 2) + (offset >> 1)
    xh = (line >> 1) ^ offset
    return (y & 3) * 4 + (xh & 1) * 2 + (rank & 1)


def columns_kernel(line_ref, b_ref, tile_ref, w_ref, o_ref, wb_ref, bias_ref, w4_ref):
    for z in range(16):
        at = source(line_ref[0], jnp.int32(z))
        rows = pl.ds(pl.multiple_of(at * 16, 16), 16)
        for g in range(8):
            v = b_ref[z, g * 16:(g + 1) * 16, :]
            o_ref[0, rows, g * 128:(g + 1) * 128] = v
            o_ref[1, rows, g * 128:(g + 1) * 128] = pltpu.roll(v.astype(jnp.float32), 64, 1).astype(jnp.bfloat16)
        wb_ref[rows, :] = b_ref[z, 128:144, :]
    bias_ref[...] = tile_ref[...]
    w4_ref[...] = w_ref[...]


def columns(line, b_all, bias, w4):
    vmem = pl.BlockSpec(memory_space=pltpu.VMEM)
    return pl.pallas_call(
        columns_kernel,
        out_shape=[jax.ShapeDtypeStruct((2, 256, 1024), jnp.bfloat16), jax.ShapeDtypeStruct((256, 128), jnp.bfloat16),
                   jax.ShapeDtypeStruct((128, 128), jnp.float32), jax.ShapeDtypeStruct((512, 256), jnp.bfloat16)],
        in_specs=[pl.BlockSpec(memory_space=pltpu.SMEM), vmem, vmem, vmem],
        out_specs=[vmem] * 4,
        compiler_params=pltpu.CompilerParams(vmem_limit_bytes=16 * 1024 * 1024),
        cost_estimate=pl.CostEstimate(flops=3*10**10, bytes_accessed=2**21, transcendentals=0),
        name="columns",
    )(line, b_all, bias, w4)


def tile(block, a_ref, b_ref, wb_ref, w_ref, bias_ref, at, xs, put):
    lane = iota((128, 128), 1)
    for g in range(8):
        t = a_ref[block, :, g * 16:(g + 1) * 16, :].reshape(256, 128).T
        for k in range(4):
            i = 4 * g + k
            row = (i % 2) * 512 + (i // 2) * 32
            at[row:row + 32, :] = t[k * 32:(k + 1) * 32, :]
    wa = a_ref[block, :, 128:144, :].reshape(256, 128)
    count = lax.dot_general(wa, wb_ref[...], (((0,), (0,)), ((), ())), preferred_element_type=jnp.float32)
    spread = count[0:8]
    for k in range(1, 4):
        spread += pltpu.roll(count[k * 8:(k + 1) * 8], 32 * (0, 2, 1, 3)[k], 1)
    inv = 1.0 / jnp.maximum(spread, 1.0)
    bias = bias_ref[...]
    low = lane < 64
    even = (lane // 32) % 2 == 0
    for n in range(4):
        for m in range(2):
            o = [jnp.dot(at[h * 512 + m * 256:h * 512 + (m + 1) * 256, :], b_ref[h, :, n * 256:(n + 1) * 256],
                         preferred_element_type=jnp.float32) for h in range(2)]
            for k in range(8):
                pair = m * 8 + k
                for t in range(2):
                    g = 2 * n + t
                    o0, o1 = (v[k * 32:(k + 1) * 32, t * 128:(t + 1) * 128] for v in o)
                    at_lane = slice((pair % 2) * 128, (pair % 2 + 1) * 128)
                    xs[0, pair // 2, g * 32:(g + 1) * 32, at_lane] = jnp.where(low[:32], o0, o1).astype(jnp.bfloat16)
                    xs[1, pair // 2, g * 32:(g + 1) * 32, at_lane] = jnp.where(low[:32], o1, o0).astype(jnp.bfloat16)
    for q in range(8):
        y = [jnp.dot(w_ref[h * 256:(h + 1) * 256, :], xs[h, q], preferred_element_type=jnp.float32) for h in range(2)]
        z = []
        for k in range(2):
            s0, s1 = (jnp.where(even, v[:128, k * 128:(k + 1) * 128], v[128:, k * 128:(k + 1) * 128]) for v in y)
            r = s0 + pltpu.roll(s1, 64, 1)
            z.append(r + pltpu.roll(r, 32 if k else 96, 1))
        put(q, ((jnp.where(even, z[0], z[1]) + bias) * inv[q:q + 1]).T)


def foreign_kernel(xl_ref, a_ref, b_ref, wb_ref, w_ref, bias_ref, o_ref, at, xs):
    def put(q, z):
        for k in range(4):
            o_ref[4 * q + (0, 2, 1, 3)[k]] = z[k * 32:(k + 1) * 32].astype(jnp.bfloat16)

    tile(1 - xl_ref[0], a_ref, b_ref, wb_ref, w_ref, bias_ref, at, xs, put)


def own_kernel(xl_ref, a_ref, b_ref, wb_ref, w_ref, bias_ref, o_ref, at, xs, held, sems):
    place = pl.ds(pl.multiple_of(xl_ref[0] * 32, 32), 32)
    copies = [pltpu.make_async_copy(held.at[pl.ds(4 * q, 4)], o_ref.at[pl.ds(4 * q, 4), place, :], sems.at[q])
              for q in range(8)]

    def put(q, z):
        for k in range(4):
            held[4 * q + (0, 2, 1, 3)[k]] = z[k * 32:(k + 1) * 32]
        copies[q].start()

    tile(xl_ref[0], a_ref, b_ref, wb_ref, w_ref, bias_ref, at, xs, put)
    for copy in copies:
        copy.wait()


def join_kernel(xl_ref, t_ref, given_ref, o_ref, held, sems):
    del given_ref
    place = pl.ds(pl.multiple_of((1 - xl_ref[0]) * 32, 32), 32)
    copies = [pltpu.make_async_copy(held.at[pl.ds(4 * q, 4)], o_ref.at[pl.ds(4 * q, 4), place, :], sems.at[q])
              for q in range(8)]
    for q in range(8):
        held[4 * q:4 * q + 4] = t_ref[4 * q:4 * q + 4].astype(jnp.float32)
        copies[q].start()
    for copy in copies:
        copy.wait()


def call(kernel, name, shape, dtype, out_space, scratch, flops, in_specs, aliases, args):
    return pl.pallas_call(
        kernel,
        out_shape=jax.ShapeDtypeStruct(shape, dtype),
        in_specs=in_specs,
        out_specs=pl.BlockSpec(memory_space=out_space),
        scratch_shapes=scratch,
        input_output_aliases=aliases,
        compiler_params=pltpu.CompilerParams(vmem_limit_bytes=24 * 1024 * 1024),
        cost_estimate=pl.CostEstimate(flops=flops, bytes_accessed=2**21, transcendentals=0),
        name=name,
    )(*args)


def shift(n, by):
    return [(i, (i + by) % n) for i in range(n)]


def places():
    out = []
    for line in range(16):
        row = []
        for z in range(16):
            dz = (z - line) % 16
            rank = 2 * min(dz, 16 - dz) - int(1 <= dz <= 8)
            y, xh = OFFSETS[rank // 2]
            row.append((line // 4 + y) % 4 * 4 + (line // 2 % 2 ^ xh) * 2 + rank % 2)
        out.append(row)
    return out


def local(x, mask, present, gain, bias, weight, proj_bias, out_weight, out_bias):
    a, b, bias2, w4 = project(x, mask, present, gain, bias, weight, proj_bias, out_bias, out_weight)
    turn = [((z * 2 + xl) * 16 + q, (at * 2 + xl) * 16 + z) for z, row in enumerate(places()) for xl in range(2)
            for at, q in enumerate(row)]
    b = lax.ppermute(b, RES + SEQ, turn)
    a_all = lax.all_to_all(a, ("xl",) + SEQ, 0, 0, tiled=True).reshape(2, 16, 144, 128)
    b_all = lax.all_gather(b, "z")
    line = sum(lax.axis_index(n) * k for n, k in zip(SEQ, (4, 2, 1))).astype(jnp.int32).reshape(1)
    b_all, wb, bias2, w4 = columns(line, b_all, bias2, w4)
    a_all, b_all = lax.optimization_barrier((a_all, b_all))

    xl = lax.axis_index("xl").astype(jnp.int32).reshape(1)
    smem, vmem, anywhere = (pl.BlockSpec(memory_space=m) for m in (pltpu.SMEM, pltpu.VMEM, pl.ANY))
    work = [pltpu.VMEM((1024, 256), jnp.bfloat16), pltpu.VMEM((2, 8, 256, 256), jnp.bfloat16)]
    held = [pltpu.VMEM((32, 32, 128), jnp.float32), pltpu.SemaphoreType.DMA((8,))]
    args, specs = (xl, a_all, b_all, wb, w4, bias2), [smem] + [vmem] * 5
    sent = call(foreign_kernel, "foreign", (32, 32, 128), jnp.bfloat16, pltpu.VMEM, work, 10**9, specs, {}, args)
    taken = lax.ppermute(sent, "xl", shift(2, 1))
    out = call(own_kernel, "own", (32, 64, 128), jnp.float32, pl.ANY, work + held, 10**9, specs, {}, args)
    return call(join_kernel, "join", (32, 64, 128), jnp.float32, pl.ANY, held, 10**6, [smem, vmem, anywhere], {2: 0},
                (xl, taken, out))


def solution(mesh):
    fine = Mesh(mesh.devices.reshape(16, 2, 4, 2, 2), RES + SEQ)
    in_specs = (P(SEQ, RES, None), P(SEQ, RES), P(RES), P(), P(), P(), P(), P(), P())
    return jax.shard_map(local, mesh=fine, in_specs=in_specs, out_specs=P(RES, SEQ, None), check_vma=False)
```
